128 devices in a mesh: grid: 16 (over z, x_lo, core), mem: 8 (over y, x_hi).
Axes of the slice: x: 4 (x_hi: 2, x_lo: 2; x = x_hi * 2 + x_lo), y: 4, z: 4, core: 2. Of those that a mesh axis runs over, the one named last changes fastest.
Arguments:
- alpha: float32 [40, 2, 1536, 768], P('mem', None, 'grid'), may hold values from -6 to 6
- perturbations: bfloat16 [40, 2, 1536, 768], P('mem', None, 'grid'), may hold values from -4.5 to 4.5
- innovation: float32 [2, 1536, 768], P(None, 'grid'), may hold values from -6.5 to 4.5
- obs_weight: float32 [2, 1536, 768], P(None, 'grid'), may hold values from 0.2 to 2
- diffusivity: float32 [2, 2], replicated, may hold values from 0.05 to 0.3, as said below
Outputs:
- gradient: float32 [40, 2, 1536, 768], P('mem', None, 'grid')
The draws below stay inside these ranges and needn't reach their ends.
Inputs may be any that keep to these rules, and one draw needn't show every extreme that they name: diffusivity[0, level] lies between 0.24 and 0.3, diffusivity[1, level] between 0.05 and 0.2.
All inputs are finite; a program needn't handle non-finite values.
Results may differ from the reference program's by a relative error of at most 0.0003.
Values sent between devices are 32-bit elements; how exact they have to be, the bound alone decides.
A program may use at most 64 MiB of HBM per device.

```python
import math
import jax
import jax.numpy as jnp
from jax import lax

NY = 768
LEV = 2
STEPS = 10
NX = 1536
MEMBERS = 40


def smooth_field(key, amplitude):
    phases = jax.random.uniform(key, (2, LEV, 1, 1), jnp.float32, 0.0, 2.0 * math.pi)
    row_place = jnp.arange(NX, dtype=jnp.float32)[None, :, None]
    column_place = jnp.arange(NY, dtype=jnp.float32)[None, None, :]
    along_rows = jnp.sin(2.0 * math.pi * row_place / 160.0 + phases[0])
    along_columns = jnp.cos(2.0 * math.pi * column_place / 230.0 + phases[1])
    return 1.0 + amplitude * along_rows * along_columns


def draw_alpha(key, part):
    key = jax.random.fold_in(key, 11)
    key_order, key_scale, key_pattern, key_rough = jax.random.split(key, 4)
    member_order = jax.random.permutation(key_order, MEMBERS)
    member_sign = jnp.where(member_order < (3 * MEMBERS + 4) // 5, 1.0, -1.0).astype(jnp.float32)
    member_scale = jax.random.uniform(key_scale, (MEMBERS,), jnp.float32, 0.7, 1.3)
    pattern = smooth_field(key_pattern, 0.4)
    rough_part = jnp.clip(jax.random.normal(key_rough, (MEMBERS, LEV, NX, NY), jnp.float32), -4.0, 4.0)
    member_factor = (member_sign * member_scale)[:, None, None, None]
    return (member_factor * pattern[None] + rough_part).astype(jnp.float32)


def draw_perturbations(key, part):
    key = jax.random.fold_in(key, 12)
    key_scale, key_pattern, key_rough = jax.random.split(key, 3)
    member_scale = jax.random.uniform(key_scale, (MEMBERS,), jnp.float32, 0.2, 0.4)
    pattern = smooth_field(key_pattern, 0.4)
    rough_part = 0.6 * jnp.clip(jax.random.normal(key_rough, (MEMBERS, LEV, NX, NY), jnp.float32), -6.0, 6.0)
    values = member_scale[:, None, None, None] * pattern[None] + rough_part
    return values.astype(jnp.bfloat16)


def draw_innovation(key, part):
    key = jax.random.fold_in(key, 13)
    key_pattern, key_rough = jax.random.split(key, 2)
    pattern = smooth_field(key_pattern, 0.4)
    rough_part = jnp.clip(jax.random.normal(key_rough, (LEV, NX, NY), jnp.float32), -5.0, 5.0)
    return (rough_part - pattern).astype(jnp.float32)


def draw_diffusivity(key, part):
    key = jax.random.fold_in(key, 14)
    key_first, key_second = jax.random.split(key, 2)
    first_rate = jax.random.uniform(key_first, (LEV,), jnp.float32, 0.24, 0.3)
    second_rate = jax.random.uniform(key_second, (LEV,), jnp.float32, 0.05, 0.2)
    return jnp.stack([first_rate, second_rate]).astype(jnp.float32)


def shard_levels(rng, extent, cuts, smallest, top_value):
    factor_of = 1.0
    for axis_at, shards_of in cuts:
        heights = jax.random.uniform(jax.random.fold_in(jax.random.fold_in(rng, 6), axis_at), (shards_of,), jnp.float32, smallest / len(cuts), top_value / len(cuts))
        factor_of = factor_of * jnp.repeat(jnp.exp(heights), extent[axis_at] // shards_of).reshape((-1,) + (1,) * (len(extent) - 1 - axis_at))
    return factor_of


def setup_inputs(seed: int = 0) -> dict:
    key_of = jax.random.split(jax.random.key(seed), 6)
    return {
        "alpha": draw_alpha(jax.random.fold_in(key_of[5], 71), 0),
        "perturbations": draw_perturbations(jax.random.fold_in(key_of[5], 71), 0),
        "innovation": draw_innovation(jax.random.fold_in(key_of[5], 71), 0),
        "obs_weight": jnp.clip(jnp.exp(math.log(2.0) - 2.3025851 * jax.random.uniform(key_of[3], (LEV, NX, NY), jnp.float32) ** shard_levels(key_of[3], (LEV, NX, NY), ((1, 16),), -0.2, 0.2)), 0.2, 2.0),
        "diffusivity": draw_diffusivity(jax.random.fold_in(key_of[5], 71), 0),
    }


def diffuse(field, diffusivity):
    kx = diffusivity[0][:, None, None]
    ky = diffusivity[1][:, None, None]
    for step in range(STEPS):
        padded = jnp.pad(field, ((0, 0), (1, 1), (1, 1)))
        along_x = padded[:, 2:, 1:-1] + padded[:, :-2, 1:-1] - 2.0 * field
        along_y = padded[:, 1:-1, 2:] + padded[:, 1:-1, :-2] - 2.0 * field
        field = field + kx * along_x + ky * along_y
    return field


def reference(alpha, perturbations, innovation, obs_weight, diffusivity):
    def accumulate(total, pair):
        control, member = pair
        return total + member.astype(jnp.float32) * diffuse(control, diffusivity), None

    start = jnp.zeros(innovation.shape, jnp.float32)
    increment, unused = lax.scan(accumulate, start, (alpha, perturbations))
    misfit = obs_weight * (increment - innovation)

    def adjoint(pair):
        control, member = pair
        return control + diffuse(member.astype(jnp.float32) * misfit, diffusivity)

    return lax.map(adjoint, (alpha, perturbations))
```

```python
import functools

import jax
import jax.numpy as jnp
import ml_dtypes
import numpy as np
from jax import lax
from jax.experimental import pallas as pl
from jax.experimental.pallas import tpu as pltpu
from jax.sharding import PartitionSpec as P

STEPS = 10
BLOCK = 128
HALO = 16
RUN = 97
PAD = 16
MESH = pl.DeviceIdType.MESH
F32 = jnp.float32
BF16 = jnp.bfloat16


def transforms(rows):
    index = np.arange(1, BLOCK + 1, dtype=np.float64)
    sine = np.sqrt(2.0 / (BLOCK + 1)) * np.sin(np.pi * np.outer(index, index) / (BLOCK + 1))
    none = np.zeros((HALO, BLOCK))
    sets = []
    for offset in (0, HALO, 2 * HALO):
        inner = sine[offset : offset + rows]
        low = sine[offset - HALO : offset] if offset else none
        high = sine[offset + rows : offset + rows + HALO] if offset < 2 * HALO else none
        wide = np.concatenate([inner, low, high])
        made = []
        for matrix in (inner, wide):
            big = matrix.astype(ml_dtypes.bfloat16)
            small = (matrix - big.astype(np.float64)).astype(ml_dtypes.bfloat16)
            nil = np.zeros_like(big)
            into = np.block([[big, small], [big, nil]])
            back = np.block([[big, big], [small, nil]])
            made.append((into, back))
        sets.append((made[0][0], made[1][1], made[1][0], made[0][1]))
    return [np.stack(each) for each in zip(*sets)], np.cos(np.pi * index / (BLOCK + 1))


def split(value):
    big = value.astype(BF16)
    return big, (value - big.astype(F32)).astype(BF16)


def march(source, target, beta, first, last, columns):
    levels = [{} for _ in range(STEPS + 1)]
    low, high, skew = -STEPS, RUN + STEPS, 1
    for front in range(low, high + STEPS * skew):
        for step in range(STEPS + 1):
            at = front - step * skew
            if step == 0:
                if at >= high:
                    continue
                value = source[pl.ds(PAD + at, 8, stride=RUN), :]
            else:
                if at - 1 < low + step - 1 or at + 1 >= high - step + 1:
                    continue
                before = levels[step - 1]
                value = (before[at - 1] + before[at + 1]) + beta * before[at]
                del before[at - 1]
            if step < STEPS:
                if at == -1:
                    value = jnp.where(first, 0.0, value)
                if at == columns - 7 * RUN:
                    value = jnp.where(last, 0.0, value)
            levels[step][at] = value
            if step == STEPS:
                target[pl.ds(at, 8, stride=RUN), :] = value


def kernel(
    tiles, groups, members, rows, columns,
    dif_ref, alpha_hbm, pert_hbm, inn_hbm, ow_hbm, w1f_hbm, w2f_hbm, w1a_hbm, w2a_hbm, cos_ref,
    out_hbm,
    alpha_v, pert_v, out_v, inn_v, ow_v, w1f, w2f, w1a, w2a,
    edge, ph, lh, part, halo_part, got, halo_got, mis, mis_halo,
    fs, gb, hb, gs, beta_v, scale_v,
    in_sem, w_sem, out_sem, ph_s, ph_r, rs_s, rs_r, rh_s, rh_r, ag_s, ag_r, ah_s, ah_r,
):
    fields = 2 * members
    g = lax.axis_index("grid")
    m = lax.axis_index("mem")
    quarter, half = m // 2, lax.rem(m, 2)
    chunk_rows, chunk_cols = rows // 4, columns // 2
    variant = (g + tiles - 2) // (tiles - 1) + g // (tiles - 1)
    has_low, has_high = g > 0, g < tiles - 1

    loads = []
    for i in range(fields):
        level, member = i // members, i % members
        loads.append(pltpu.make_async_copy(pert_hbm.at[member, level], pert_v.at[i], in_sem.at[0, i]))
    for i in range(fields):
        level, member = i // members, i % members
        loads.append(pltpu.make_async_copy(alpha_hbm.at[member, level], alpha_v.at[i], in_sem.at[1, i]))
    weights = []
    for n, (src, dst) in enumerate(((w1f_hbm, w1f), (w2f_hbm, w2f), (w1a_hbm, w1a), (w2a_hbm, w2a))):
        weights.append(pltpu.make_async_copy(src.at[variant], dst, w_sem.at[n]))
    r0 = pl.multiple_of(quarter * chunk_rows, 8)
    c0 = pl.multiple_of(half * chunk_cols, 128)
    window = (slice(None), pl.ds(r0, chunk_rows), pl.ds(c0, chunk_cols))
    weights.append(pltpu.make_async_copy(inn_hbm.at[window], inn_v, w_sem.at[4]))
    weights.append(pltpu.make_async_copy(ow_hbm.at[window], ow_v, w_sem.at[5]))
    for copy in loads[:fields] + weights[:4] + loads[fields:] + weights[4:]:
        copy.start()

    barrier = pltpu.get_barrier_semaphore()
    for k in range(1, groups):
        pl.semaphore_signal(barrier, 1, device_id=(g, lax.rem(m + k, groups)), device_id_type=MESH)

    @pl.when(has_low)
    def _():
        for p in range(groups):
            pl.semaphore_signal(barrier, 1, device_id=(g - 1, p), device_id_type=MESH)

    @pl.when(has_high)
    def _():
        for p in range(groups):
            pl.semaphore_signal(barrier, 1, device_id=(g + 1, p), device_id_type=MESH)

    part[...] = jnp.zeros_like(part)
    halo_part[...] = jnp.zeros_like(halo_part)
    for level in range(2):
        kx = jnp.full((8, BLOCK), dif_ref[0, level], F32)
        ky = jnp.full((8, BLOCK), dif_ref[1, level], F32)
        beta_v[level] = (1.0 - 2.0 * ky - 2.0 * kx + 2.0 * kx * cos_ref[...]) / ky
        square = ky * ky
        fourth = square * square
        scale_v[level] = fourth * fourth * square
    gb[...] = jnp.zeros_like(gb)

    @pl.when(g == 0)
    def _():
        ph[0] = jnp.zeros_like(ph[0])
        mis_halo[:, 0] = jnp.zeros_like(mis_halo[:, 0])

    @pl.when(g == tiles - 1)
    def _():
        ph[1] = jnp.zeros_like(ph[1])
        mis_halo[:, 1] = jnp.zeros_like(mis_halo[:, 1])

    for i in range(fields):
        loads[i].wait()
        edge[1, i] = pert_v[i, 0:HALO, :].astype(F32)
        edge[0, i] = pert_v[i, rows - HALO : rows, :].astype(F32)

    neighbours = jnp.minimum(g, 1) + jnp.minimum(tiles - 1 - g, 1)
    pl.semaphore_wait(barrier, groups - 1 + groups * neighbours)

    def edge_copy(level, side):
        piece = pl.ds(level * members, members)
        return pltpu.make_async_remote_copy(
            src_ref=edge.at[side, piece], dst_ref=ph.at[side, piece],
            send_sem=ph_s.at[level, side], recv_sem=ph_r.at[level, side],
            device_id=(g + 1 - 2 * side, m), device_id_type=MESH,
        )

    for level in range(2):

        @pl.when(has_high)
        def _():
            edge_copy(level, 0).start()

        @pl.when(has_low)
        def _():
            edge_copy(level, 1).start()

    for copy in weights:
        copy.wait()

    def rs_copy(level, k):
        peer = lax.rem(m + k, groups)
        return pltpu.make_async_remote_copy(
            src_ref=part.at[level, peer], dst_ref=got.at[level, m],
            send_sem=rs_s.at[level, k], recv_sem=rs_r.at[level, m],
            device_id=(g, peer), device_id_type=MESH,
        )

    def rh_copy(level, side, h):
        return pltpu.make_async_remote_copy(
            src_ref=halo_part.at[level, side, h], dst_ref=halo_got.at[level, m],
            send_sem=rh_s.at[level, side, h], recv_sem=rh_r.at[level, m],
            device_id=(g - 1 + 2 * side, (groups - 2) * (1 - side) + h), device_id_type=MESH,
        )

    def ag_copy(level, k):
        return pltpu.make_async_remote_copy(
            src_ref=mis.at[level, m], dst_ref=mis.at[level, m],
            send_sem=ag_s.at[level, k], recv_sem=ag_r.at[level, m],
            device_id=(g, lax.rem(m + k, groups)), device_id_type=MESH,
        )

    def ah_copy(level, side, p):
        first = (chunk_rows - HALO) * (1 - side)
        return pltpu.make_async_remote_copy(
            src_ref=mis.at[level, m, pl.ds(first, HALO)], dst_ref=mis_halo.at[level, side, half],
            send_sem=ah_s.at[level, side, p], recv_sem=ah_r.at[level, side, half],
            device_id=(g + 1 - 2 * side, p), device_id_type=MESH,
        )

    def landed(ref, sem):
        pltpu.make_async_copy(ref, ref, sem).wait()

    def send_sums(level):
        @pl.when(has_low)
        def _():
            landed(ph.at[0, pl.ds(level * members, members)], ph_r.at[level, 0])

        @pl.when(has_high)
        def _():
            landed(ph.at[1, pl.ds(level * members, members)], ph_r.at[level, 1])

        for h in range(2):
            cut = slice(h * chunk_cols, (h + 1) * chunk_cols)
            for side in range(2):
                total = None
                for f in range(members):
                    i = level * members + f
                    term = lh[i, side, :, cut] * ph[side, i, :, cut]
                    total = term if total is None else total + term
                halo_part[level, side, h] = total
        for k in range(1, groups):
            rs_copy(level, k).start()

        @pl.when(has_low)
        def _():
            for h in range(2):
                rh_copy(level, 0, h).start()

        @pl.when(has_high)
        def _():
            for h in range(2):
                rh_copy(level, 1, h).start()

    at_low = (quarter == 0) & has_low
    at_high = (quarter == 3) & has_high

    def send_misfit(level):
        for k in range(1, groups):
            p = lax.rem(m + k, groups)
            landed(got.at[level, p], rs_r.at[level, p])
        total = part[level, m]
        for k in range(1, groups):
            total = total + got[level, lax.rem(m + k, groups)]
        got[level, m] = total

        @pl.when(at_low)
        def _():
            for p in range(groups):
                landed(halo_got.at[level, p], rh_r.at[level, p])
            got[level, m, 0:HALO] = got[level, m, 0:HALO] + sum(halo_got[level, p] for p in range(groups))

        @pl.when(at_high)
        def _():
            for p in range(groups):
                landed(halo_got.at[level, p], rh_r.at[level, p])
            last = slice(chunk_rows - HALO, chunk_rows)
            got[level, m, last] = got[level, m, last] + sum(halo_got[level, p] for p in range(groups))

        scale = scale_v[level, 0:1, 0:1]
        mis[level, m] = ow_v[level] * (got[level, m] * scale - inn_v[level]) * scale
        for k in range(1, groups):
            ag_copy(level, k).start()

        @pl.when(at_low)
        def _():
            for p in range(groups):
                ah_copy(level, 1, p).start()

        @pl.when(at_high)
        def _():
            for p in range(groups):
                ah_copy(level, 0, p).start()

    def take_misfit(level):
        for k in range(1, groups):
            p = lax.rem(m + k, groups)
            landed(mis.at[level, p], ag_r.at[level, p])

        @pl.when(has_low)
        def _():
            for h in range(2):
                landed(mis_halo.at[level, 0, h], ah_r.at[level, 0, h])

        @pl.when(has_high)
        def _():
            for h in range(2):
                landed(mis_halo.at[level, 1, h], ah_r.at[level, 1, h])

    sub = lax.broadcasted_iota(jnp.int32, (8, BLOCK), 0)
    first, last = sub == 0, sub == 7
    wide = 256

    def to_modes(count, weight):
        for c in range(0, columns, wide):
            made = lax.dot_general(
                fs[0:count, c : c + wide], weight[...], (((0,), (0,)), ((), ())), preferred_element_type=F32
            )
            gb[PAD + c : PAD + c + wide, :] = made[:, :BLOCK] + made[:, BLOCK:]

    def modes_out():
        for c in range(0, columns, 128):
            big, small = split(hb[c : c + 128, :])
            gs[c : c + 128, 0:BLOCK] = big
            gs[c : c + 128, BLOCK:] = small

    def from_modes(weight, c):
        return lax.dot_general(
            weight[...], gs[c : c + wide, :], (((1,), (1,)), ((), ())), preferred_element_type=F32
        )

    def forward(i, carry):
        level = i // members
        pltpu.make_async_copy(alpha_hbm.at[0, 0], alpha_v.at[i], in_sem.at[1, i]).wait()
        for c in range(0, columns, 128):
            big, small = split(alpha_v[i, :, c : c + 128])
            fs[0:rows, c : c + 128] = big
            fs[rows : 2 * rows, c : c + 128] = small
        to_modes(2 * rows, w1f)
        march(gb, hb, beta_v[level], first, last, columns)
        modes_out()
        for c in range(0, columns, wide):
            made = from_modes(w2f, c)
            made = made[:BLOCK] + made[BLOCK:]
            lh[i, 0, :, c : c + wide] = made[rows : rows + HALO]
            lh[i, 1, :, c : c + wide] = made[rows + HALO :]
            for d in range(c, c + wide, 128):
                h, e = d // chunk_cols, d % chunk_cols
                term = made[:rows, d - c : d - c + 128] * pert_v[i, :, d : d + 128].astype(F32)
                for q in range(4):
                    spot = (level, 2 * q + h, slice(None), slice(e, e + 128))
                    part[spot] = part[spot] + term[q * chunk_rows : (q + 1) * chunk_rows]

        @pl.when(i == members - 1)
        def _():
            send_sums(0)

        @pl.when(i == fields - 2)
        def _():
            send_misfit(0)

        return carry

    lax.fori_loop(0, fields, forward, 0)
    send_sums(1)

    def adjoint(i, carry):
        level = i // members

        @pl.when(i == 0)
        def _():
            take_misfit(0)

        @pl.when(i == members - 2)
        def _():
            send_misfit(1)

        @pl.when(i == members)
        def _():
            take_misfit(1)

        for c in range(0, columns, 128):
            h, e = c // chunk_cols, c % chunk_cols
            weightless = pert_v[i, :, c : c + 128].astype(F32)
            pieces = []
            for q in range(4):
                pieces.append(
                    weightless[q * chunk_rows : (q + 1) * chunk_rows] * mis[level, 2 * q + h, :, e : e + 128]
                )
            for side in range(2):
                pieces.append(ph[side, i, :, c : c + 128] * mis_halo[level, side, h, :, e : e + 128])
            big, small = split(jnp.concatenate(pieces, axis=0))
            fs[0:BLOCK, c : c + 128] = big
            fs[BLOCK : 2 * BLOCK, c : c + 128] = small
        to_modes(2 * BLOCK, w1a)
        march(gb, hb, beta_v[level], first, last, columns)
        modes_out()
        for c in range(0, columns, wide):
            made = from_modes(w2a, c)
            out_v[i, :, c : c + wide] = alpha_v[i, :, c : c + wide] + (made[:rows] + made[rows:])
        pltpu.make_async_copy(out_v.at[i], out_hbm.at[lax.rem(i, members), level], out_sem.at[i]).start()
        return carry

    lax.fori_loop(0, fields, adjoint, 0)

    for i in range(fields):
        pltpu.make_async_copy(out_v.at[i], out_hbm.at[i % members, i // members], out_sem.at[i]).wait()
    for level in range(2):
        for k in range(1, groups):
            rs_copy(level, k).wait_send()
            ag_copy(level, k).wait_send()

        @pl.when(has_low)
        def _():
            edge_copy(level, 1).wait_send()
            for h in range(2):
                rh_copy(level, 0, h).wait_send()

        @pl.when(has_high)
        def _():
            edge_copy(level, 0).wait_send()
            for h in range(2):
                rh_copy(level, 1, h).wait_send()

        @pl.when(at_low)
        def _():
            for p in range(groups):
                ah_copy(level, 1, p).wait_send()

        @pl.when(at_high)
        def _():
            for p in range(groups):
                ah_copy(level, 0, p).wait_send()


def local(tiles, groups, alpha, perturbations, innovation, obs_weight, diffusivity):
    members, levels, rows, columns = alpha.shape
    fields = members * levels
    (w1f, w2f, w1a, w2a), cosine = transforms(rows)
    cosine = np.broadcast_to(cosine.astype(np.float32), (8, BLOCK))
    any_space = pl.BlockSpec(memory_space=pl.ANY)
    dma = pltpu.SemaphoreType.DMA
    chunk = (rows // 4, columns // 2)
    halo = (HALO, columns // 2)
    return pl.pallas_call(
        functools.partial(kernel, tiles, groups, members, rows, columns),
        out_shape=jax.ShapeDtypeStruct(alpha.shape, F32),
        in_specs=[pl.BlockSpec(memory_space=pltpu.SMEM)] + [any_space] * 8 + [pl.BlockSpec(memory_space=pltpu.VMEM)],
        out_specs=any_space,
        scratch_shapes=[
            pltpu.VMEM((fields, rows, columns), F32),
            pltpu.VMEM((fields, rows, columns), BF16),
            pltpu.VMEM((fields, rows, columns), F32),
            pltpu.VMEM((levels,) + chunk, F32),
            pltpu.VMEM((levels,) + chunk, F32),
            pltpu.VMEM(w1f.shape[1:], BF16),
            pltpu.VMEM(w2f.shape[1:], BF16),
            pltpu.VMEM(w1a.shape[1:], BF16),
            pltpu.VMEM(w2a.shape[1:], BF16),
            pltpu.VMEM((2, fields, HALO, columns), F32),
            pltpu.VMEM((2, fields, HALO, columns), F32),
            pltpu.VMEM((fields, 2, HALO, columns), F32),
            pltpu.VMEM((levels, groups) + chunk, F32),
            pltpu.VMEM((levels, 2, 2) + halo, F32),
            pltpu.VMEM((levels, groups) + chunk, F32),
            pltpu.VMEM((levels, groups) + halo, F32),
            pltpu.VMEM((levels, groups) + chunk, F32),
            pltpu.VMEM((levels, 2, 2) + halo, F32),
            pltpu.VMEM((2 * BLOCK, columns), BF16),
            pltpu.VMEM((PAD + 8 * RUN + PAD, BLOCK), F32),
            pltpu.VMEM((8 * RUN, BLOCK), F32),
            pltpu.VMEM((8 * RUN, 2 * BLOCK), BF16),
            pltpu.VMEM((levels, 8, BLOCK), F32),
            pltpu.VMEM((levels, 8, BLOCK), F32),
            dma((2, fields)),
            dma((6,)),
            dma((fields,)),
            dma((levels, 2)),
            dma((levels, 2)),
            dma((levels, groups)),
            dma((levels, groups)),
            dma((levels, 2, 2)),
            dma((levels, groups)),
            dma((levels, groups)),
            dma((levels, groups)),
            dma((levels, 2, groups)),
            dma((levels, 2, 2)),
        ],
        compiler_params=pltpu.CompilerParams(
            collective_id=0, has_side_effects=True, vmem_limit_bytes=48 * 2**20
        ),
    )(diffusivity, alpha, perturbations, innovation, obs_weight, w1f, w2f, w1a, w2a, cosine)


def solution(mesh):
    in_specs = (
        P("mem", None, "grid", None),
        P("mem", None, "grid", None),
        P(None, "grid", None),
        P(None, "grid", None),
        P(),
    )
    out_specs = P("mem", None, "grid", None)
    body = functools.partial(local, mesh.shape["grid"], mesh.shape["mem"])
    return jax.shard_map(body, mesh=mesh, in_specs=in_specs, out_specs=out_specs, check_vma=False)
```

```python
import functools

import jax
import jax.numpy as jnp
import ml_dtypes
import numpy as np
from jax import lax
from jax.experimental import pallas as pl
from jax.experimental.pallas import tpu as pltpu
from jax.sharding import PartitionSpec as P

STEPS = 10
BLOCK = 128
HALO = 16
RUN = 97
PAD = 16
MESH = pl.DeviceIdType.MESH
F32 = jnp.float32
BF16 = jnp.bfloat16


def transforms(rows):
    index = np.arange(1, BLOCK + 1, dtype=np.float64)
    sine = np.sqrt(2.0 / (BLOCK + 1)) * np.sin(np.pi * np.outer(index, index) / (BLOCK + 1))
    none = np.zeros((HALO, BLOCK))
    sets = []
    for offset in (0, HALO, 2 * HALO):
        inner = sine[offset : offset + rows]
        low = sine[offset - HALO : offset] if offset else none
        high = sine[offset + rows : offset + rows + HALO] if offset < 2 * HALO else none
        wide = np.concatenate([inner, low, high])
        made = []
        for matrix in (inner, wide):
            big = matrix.astype(ml_dtypes.bfloat16)
            small = (matrix - big.astype(np.float64)).astype(ml_dtypes.bfloat16)
            nil = np.zeros_like(big)
            into = np.block([[big, small], [big, nil]])
            back = np.block([[big, big], [small, nil]])
            made.append((into, back))
        sets.append((made[0][0], made[1][1], made[1][0], made[0][1]))
    return [np.stack(each) for each in zip(*sets)], np.cos(np.pi * index / (BLOCK + 1))


def split(value):
    big = value.astype(BF16)
    return big, (value - big.astype(F32)).astype(BF16)


def march(source, target, beta, first, last, columns):
    levels = [{} for _ in range(STEPS + 1)]
    low, high, skew = -STEPS, RUN + STEPS, 1
    for front in range(low, high + STEPS * skew):
        for step in range(STEPS + 1):
            at = front - step * skew
            if step == 0:
                if at >= high:
                    continue
                value = source[pl.ds(PAD + at, 8, stride=RUN), :]
            else:
                if at - 1 < low + step - 1 or at + 1 >= high - step + 1:
                    continue
                before = levels[step - 1]
                value = (before[at - 1] + before[at + 1]) + beta * before[at]
                del before[at - 1]
            if step < STEPS:
                if at == -1:
                    value = jnp.where(first, 0.0, value)
                if at == columns - 7 * RUN:
                    value = jnp.where(last, 0.0, value)
            levels[step][at] = value
            if step == STEPS:
                target[pl.ds(at, 8, stride=RUN), :] = value


def kernel(
    tiles, groups, members, rows, columns,
    dif_ref, alpha_hbm, pert_hbm, inn_hbm, ow_hbm, w1f_hbm, w2f_hbm, w1a_hbm, w2a_hbm, cos_hbm,
    out_hbm,
    alpha_v, pert_v, out_v, inn_v, ow_v, cos_ref, w1f, w2f, w1a, w2a,
    edge, edge_got, ph, lh, part, halo_part, got, halo_got, mis, mis_halo,
    fs, gb, hb, gs, beta_v, scale_v,
    in_sem, w_sem, out_sem, ph_s, ph_r, rs_s, rs_r, rh_s, rh_r, ag_s, ag_r, ah_s, ah_r,
):
    fields = 2 * members
    g = lax.axis_index("grid")
    m = lax.axis_index("mem")
    quarter, half = m // 2, lax.rem(m, 2)
    chunk_rows, chunk_cols = rows // 4, columns // 2
    variant = (g + tiles - 2) // (tiles - 1) + g // (tiles - 1)
    has_low, has_high = g > 0, g < tiles - 1

    loads = []
    for i in range(fields):
        level, member = i // members, i % members
        loads.append(pltpu.make_async_copy(pert_hbm.at[member, level], pert_v.at[i], in_sem.at[0, i]))
    for i in range(fields):
        level, member = i // members, i % members
        loads.append(pltpu.make_async_copy(alpha_hbm.at[member, level], alpha_v.at[i], in_sem.at[1, i]))
    cosines = pltpu.make_async_copy(cos_hbm, cos_ref, w_sem.at[6])
    weights = []
    for n, (src, dst) in enumerate(((w1f_hbm, w1f), (w2f_hbm, w2f), (w1a_hbm, w1a), (w2a_hbm, w2a))):
        weights.append(pltpu.make_async_copy(src.at[variant], dst, w_sem.at[n]))
    r0 = pl.multiple_of(quarter * chunk_rows, 8)
    c0 = pl.multiple_of(half * chunk_cols, 128)
    window = (slice(None), pl.ds(r0, chunk_rows), pl.ds(c0, chunk_cols))
    weights.append(pltpu.make_async_copy(inn_hbm.at[window], inn_v, w_sem.at[4]))
    weights.append(pltpu.make_async_copy(ow_hbm.at[window], ow_v, w_sem.at[5]))
    for copy in loads[:fields] + [cosines] + loads[fields : fields + 1] + weights[:4] + loads[fields + 1 :] + weights[4:]:
        copy.start()

    barrier = pltpu.get_barrier_semaphore()
    for k in range(1, groups):
        pl.semaphore_signal(barrier, 1, device_id=(g, lax.rem(m + k, groups)), device_id_type=MESH)

    @pl.when(has_low)
    def _():
        pl.semaphore_signal(barrier, 1, device_id=(g - 1, m), device_id_type=MESH)

    @pl.when(has_high)
    def _():
        pl.semaphore_signal(barrier, 1, device_id=(g + 1, m), device_id_type=MESH)

    part[...] = jnp.zeros_like(part)
    cosines.wait()
    for level in range(2):
        kx = jnp.full((8, BLOCK), dif_ref[0, level], F32)
        ky = jnp.full((8, BLOCK), dif_ref[1, level], F32)
        beta_v[level] = (1.0 - 2.0 * ky - 2.0 * kx + 2.0 * kx * cos_ref[...]) / ky
        square = ky * ky
        fourth = square * square
        scale_v[level] = fourth * fourth * square
    gb[...] = jnp.zeros_like(gb)
    ph[...] = jnp.zeros_like(ph)

    @pl.when(g == 0)
    def _():
        mis_halo[:, 0] = jnp.zeros_like(mis_halo[:, 0])

    @pl.when(g == tiles - 1)
    def _():
        mis_halo[:, 1] = jnp.zeros_like(mis_halo[:, 1])

    for i in range(fields):
        loads[i].wait()
        level, at = i // members, STEPS * (i % members)
        edge[1, level, at : at + STEPS] = pert_v[i, 0:HALO, :].astype(F32)[:STEPS]
        edge[0, level, at : at + STEPS] = pert_v[i, rows - HALO : rows, :].astype(F32)[HALO - STEPS :]

    def edge_copy(level, side):
        return pltpu.make_async_remote_copy(
            src_ref=edge.at[side, level], dst_ref=edge_got.at[side, level],
            send_sem=ph_s.at[level, side], recv_sem=ph_r.at[level, side],
            device_id=(g + 1 - 2 * side, m), device_id_type=MESH,
        )

    def send_edges(level):
        @pl.when(has_high)
        def _():
            edge_copy(level, 0).start()

        @pl.when(has_low)
        def _():
            edge_copy(level, 1).start()

    def edges_sent(level):
        @pl.when(has_high)
        def _():
            edge_copy(level, 0).wait_send()

        @pl.when(has_low)
        def _():
            edge_copy(level, 1).wait_send()

    def start_exchange():
        neighbours = jnp.minimum(g, 1) + jnp.minimum(tiles - 1 - g, 1)
        pl.semaphore_wait(barrier, groups - 1 + neighbours)
        send_edges(0)

    for copy in weights:
        copy.wait()

    def rs_copy(level, k):
        peer = lax.rem(m + k, groups)
        return pltpu.make_async_remote_copy(
            src_ref=part.at[level, peer], dst_ref=got.at[level, m],
            send_sem=rs_s.at[level, k], recv_sem=rs_r.at[level, m],
            device_id=(g, peer), device_id_type=MESH,
        )

    def rh_copy(level, side, h):
        return pltpu.make_async_remote_copy(
            src_ref=halo_part.at[level, side, h], dst_ref=halo_got.at[level, m],
            send_sem=rh_s.at[level, side, h], recv_sem=rh_r.at[level, m],
            device_id=(g - 1 + 2 * side, (groups - 2) * (1 - side) + h), device_id_type=MESH,
        )

    def ag_copy(level, k):
        return pltpu.make_async_remote_copy(
            src_ref=mis.at[level, m], dst_ref=mis.at[level, m],
            send_sem=ag_s.at[level, k], recv_sem=ag_r.at[level, m],
            device_id=(g, lax.rem(m + k, groups)), device_id_type=MESH,
        )

    def ah_copy(level, side, p):
        first = (chunk_rows - HALO) * (1 - side)
        return pltpu.make_async_remote_copy(
            src_ref=mis.at[level, m, pl.ds(first, HALO)], dst_ref=mis_halo.at[level, side, half],
            send_sem=ah_s.at[level, side, p], recv_sem=ah_r.at[level, side, half],
            device_id=(g + 1 - 2 * side, p), device_id_type=MESH,
        )

    def landed(ref, sem):
        pltpu.make_async_copy(ref, ref, sem).wait()

    def send_sums(level):
        for k in range(1, groups):
            rs_copy(level, k).start()

    def send_halo_sums(level):
        for side, there in ((0, has_low), (1, has_high)):

            @pl.when(there)
            def _():
                landed(edge_got.at[side, level], ph_r.at[level, side])
                for f in range(members):
                    value = edge_got[side, level, f * STEPS : (f + 1) * STEPS]
                    start = (HALO - STEPS) * (1 - side)
                    ph[side, level * members + f, start : start + STEPS] = value
                for h in range(2):
                    cut = slice(h * chunk_cols, (h + 1) * chunk_cols)
                    total = None
                    for f in range(members):
                        i = level * members + f
                        term = lh[i, side, :, cut] * ph[side, i, :, cut]
                        total = term if total is None else total + term
                    halo_part[level, side, h] = total
                for h in range(2):
                    rh_copy(level, side, h).start()

    at_low = (quarter == 0) & has_low
    at_high = (quarter == 3) & has_high

    def send_misfit(level):
        for k in range(1, groups):
            p = lax.rem(m + k, groups)
            landed(got.at[level, p], rs_r.at[level, p])
        total = part[level, m]
        for k in range(1, groups):
            total = total + got[level, lax.rem(m + k, groups)]
        got[level, m] = total

        @pl.when(at_low)
        def _():
            for p in range(groups):
                landed(halo_got.at[level, p], rh_r.at[level, p])
            got[level, m, 0:HALO] = got[level, m, 0:HALO] + sum(halo_got[level, p] for p in range(groups))

        @pl.when(at_high)
        def _():
            for p in range(groups):
                landed(halo_got.at[level, p], rh_r.at[level, p])
            last = slice(chunk_rows - HALO, chunk_rows)
            got[level, m, last] = got[level, m, last] + sum(halo_got[level, p] for p in range(groups))

        scale = scale_v[level, 0:1, 0:1]
        mis[level, m] = ow_v[level] * (got[level, m] * scale - inn_v[level]) * scale
        for k in range(1, groups):
            ag_copy(level, k).start()

        @pl.when(at_low)
        def _():
            for p in range(groups):
                ah_copy(level, 1, p).start()

        @pl.when(at_high)
        def _():
            for p in range(groups):
                ah_copy(level, 0, p).start()

    def take_misfit(level):
        for k in range(1, groups):
            p = lax.rem(m + k, groups)
            landed(mis.at[level, p], ag_r.at[level, p])

        @pl.when(has_low)
        def _():
            for h in range(2):
                landed(mis_halo.at[level, 0, h], ah_r.at[level, 0, h])

        @pl.when(has_high)
        def _():
            for h in range(2):
                landed(mis_halo.at[level, 1, h], ah_r.at[level, 1, h])

    sub = lax.broadcasted_iota(jnp.int32, (8, BLOCK), 0)
    first, last = sub == 0, sub == 7
    wide = 256

    def to_modes(count, weight):
        for c in range(0, columns, wide):
            made = lax.dot_general(
                fs[0:count, c : c + wide], weight[...], (((0,), (0,)), ((), ())), preferred_element_type=F32
            )
            gb[PAD + c : PAD + c + wide, :] = made[:, :BLOCK] + made[:, BLOCK:]

    def modes_out():
        for c in range(0, columns, 128):
            big, small = split(hb[c : c + 128, :])
            gs[c : c + 128, 0:BLOCK] = big
            gs[c : c + 128, BLOCK:] = small

    def from_modes(weight, c):
        return lax.dot_general(
            weight[...], gs[c : c + wide, :], (((1,), (1,)), ((), ())), preferred_element_type=F32
        )

    def forward(i, carry):
        level = i // members
        pltpu.make_async_copy(alpha_hbm.at[0, 0], alpha_v.at[i], in_sem.at[1, i]).wait()
        for c in range(0, columns, 128):
            big, small = split(alpha_v[i, :, c : c + 128])
            fs[0:rows, c : c + 128] = big
            fs[rows : 2 * rows, c : c + 128] = small
        to_modes(2 * rows, w1f)
        march(gb, hb, beta_v[level], first, last, columns)
        modes_out()
        for c in range(0, columns, wide):
            made = from_modes(w2f, c)
            made = made[:BLOCK] + made[BLOCK:]
            lh[i, 0, :, c : c + wide] = made[rows : rows + HALO]
            lh[i, 1, :, c : c + wide] = made[rows + HALO :]
            for d in range(c, c + wide, 128):
                h, e = d // chunk_cols, d % chunk_cols
                term = made[:rows, d - c : d - c + 128] * pert_v[i, :, d : d + 128].astype(F32)
                for q in range(4):
                    spot = (level, 2 * q + h, slice(None), slice(e, e + 128))
                    part[spot] = part[spot] + term[q * chunk_rows : (q + 1) * chunk_rows]

        @pl.when(i == 0)
        def _():
            start_exchange()

        @pl.when(i == members - 2)
        def _():
            edges_sent(0)
            send_edges(1)

        @pl.when(i == members - 1)
        def _():
            send_sums(0)

        @pl.when(i == members + 1)
        def _():
            send_halo_sums(0)

        return carry

    lax.fori_loop(0, fields, forward, 0)
    send_sums(1)
    send_halo_sums(1)
    send_misfit(0)
    send_misfit(1)
    edges_sent(1)

    def adjoint(i, carry):
        level = i // members

        @pl.when(i == 0)
        def _():
            take_misfit(0)

        @pl.when(i == members)
        def _():
            take_misfit(1)

        for c in range(0, columns, 128):
            h, e = c // chunk_cols, c % chunk_cols
            weightless = pert_v[i, :, c : c + 128].astype(F32)
            pieces = []
            for q in range(4):
                pieces.append(
                    weightless[q * chunk_rows : (q + 1) * chunk_rows] * mis[level, 2 * q + h, :, e : e + 128]
                )
            for side in range(2):
                pieces.append(ph[side, i, :, c : c + 128] * mis_halo[level, side, h, :, e : e + 128])
            big, small = split(jnp.concatenate(pieces, axis=0))
            fs[0:BLOCK, c : c + 128] = big
            fs[BLOCK : 2 * BLOCK, c : c + 128] = small
        to_modes(2 * BLOCK, w1a)
        march(gb, hb, beta_v[level], first, last, columns)
        modes_out()
        for c in range(0, columns, wide):
            made = from_modes(w2a, c)
            out_v[i, :, c : c + wide] = alpha_v[i, :, c : c + wide] + (made[:rows] + made[rows:])
        pltpu.make_async_copy(out_v.at[i], out_hbm.at[lax.rem(i, members), level], out_sem.at[i]).start()
        return carry

    lax.fori_loop(0, fields, adjoint, 0)

    for i in range(fields):
        pltpu.make_async_copy(out_v.at[i], out_hbm.at[i % members, i // members], out_sem.at[i]).wait()
    for level in range(2):
        for k in range(1, groups):
            rs_copy(level, k).wait_send()
            ag_copy(level, k).wait_send()

        @pl.when(has_low)
        def _():
            for h in range(2):
                rh_copy(level, 0, h).wait_send()

        @pl.when(has_high)
        def _():
            for h in range(2):
                rh_copy(level, 1, h).wait_send()

        @pl.when(at_low)
        def _():
            for p in range(groups):
                ah_copy(level, 1, p).wait_send()

        @pl.when(at_high)
        def _():
            for p in range(groups):
                ah_copy(level, 0, p).wait_send()


def local(tiles, groups, alpha, perturbations, innovation, obs_weight, diffusivity):
    members, levels, rows, columns = alpha.shape
    fields = members * levels
    (w1f, w2f, w1a, w2a), cosine = transforms(rows)
    cosine = np.broadcast_to(cosine.astype(np.float32), (8, BLOCK))
    any_space = pl.BlockSpec(memory_space=pltpu.HBM)
    dma = pltpu.SemaphoreType.DMA
    chunk = (rows // 4, columns // 2)
    halo = (HALO, columns // 2)
    packed = -(-STEPS * members // 8) * 8
    return pl.pallas_call(
        functools.partial(kernel, tiles, groups, members, rows, columns),
        out_shape=jax.ShapeDtypeStruct(alpha.shape, F32),
        in_specs=[pl.BlockSpec(memory_space=pltpu.SMEM)] + [any_space] * 9,
        out_specs=any_space,
        scratch_shapes=[
            pltpu.VMEM((fields, rows, columns), F32),
            pltpu.VMEM((fields, rows, columns), BF16),
            pltpu.VMEM((fields, rows, columns), F32),
            pltpu.VMEM((levels,) + chunk, F32),
            pltpu.VMEM((levels,) + chunk, F32),
            pltpu.VMEM(cosine.shape, F32),
            pltpu.VMEM(w1f.shape[1:], BF16),
            pltpu.VMEM(w2f.shape[1:], BF16),
            pltpu.VMEM(w1a.shape[1:], BF16),
            pltpu.VMEM(w2a.shape[1:], BF16),
            pltpu.VMEM((2, levels, packed, columns), F32),
            pltpu.VMEM((2, levels, packed, columns), F32),
            pltpu.VMEM((2, fields, HALO, columns), F32),
            pltpu.VMEM((fields, 2, HALO, columns), F32),
            pltpu.VMEM((levels, groups) + chunk, F32),
            pltpu.VMEM((levels, 2, 2) + halo, F32),
            pltpu.VMEM((levels, groups) + chunk, F32),
            pltpu.VMEM((levels, groups) + halo, F32),
            pltpu.VMEM((levels, groups) + chunk, F32),
            pltpu.VMEM((levels, 2, 2) + halo, F32),
            pltpu.VMEM((2 * BLOCK, columns), BF16),
            pltpu.VMEM((PAD + 8 * RUN + PAD, BLOCK), F32),
            pltpu.VMEM((8 * RUN, BLOCK), F32),
            pltpu.VMEM((8 * RUN, 2 * BLOCK), BF16),
            pltpu.VMEM((levels, 8, BLOCK), F32),
            pltpu.VMEM((levels, 8, BLOCK), F32),
            dma((2, fields)),
            dma((7,)),
            dma((fields,)),
            dma((levels, 2)),
            dma((levels, 2)),
            dma((levels, groups)),
            dma((levels, groups)),
            dma((levels, 2, 2)),
            dma((levels, groups)),
            dma((levels, groups)),
            dma((levels, groups)),
            dma((levels, 2, groups)),
            dma((levels, 2, 2)),
        ],
        compiler_params=pltpu.CompilerParams(
            collective_id=0, has_side_effects=True, vmem_limit_bytes=60 * 2**20
        ),
    )(diffusivity, alpha, perturbations, innovation, obs_weight, w1f, w2f, w1a, w2a, cosine)


def solution(mesh):
    in_specs = (
        P("mem", None, "grid", None),
        P("mem", None, "grid", None),
        P(None, "grid", None),
        P(None, "grid", None),
        P(),
    )
    out_specs = P("mem", None, "grid", None)
    body = functools.partial(local, mesh.shape["grid"], mesh.shape["mem"])
    return jax.shard_map(body, mesh=mesh, in_specs=in_specs, out_specs=out_specs, check_vma=False)
```

```python
import functools

import jax
import jax.numpy as jnp
import ml_dtypes
import numpy as np
from jax import lax
from jax.experimental import pallas as pl
from jax.experimental.pallas import tpu as pltpu
from jax.sharding import PartitionSpec as P

STEPS = 10
UNROLL = 5
BLOCK = 128
HALO = 16
RUN = 97
PAD = 16
MESH = pl.DeviceIdType.MESH
F32 = jnp.float32
BF16 = jnp.bfloat16


def transforms(rows):
    index = np.arange(1, BLOCK + 1, dtype=np.float64)
    sine = np.sqrt(2.0 / (BLOCK + 1)) * np.sin(np.pi * np.outer(index, index) / (BLOCK + 1))
    none = np.zeros((HALO, BLOCK))
    sets = []
    for offset in (0, HALO, 2 * HALO):
        inner = sine[offset : offset + rows]
        low = sine[offset - HALO : offset] if offset else none
        high = sine[offset + rows : offset + rows + HALO] if offset < 2 * HALO else none
        wide = np.concatenate([inner, low, high])
        made = []
        for matrix in (inner, wide):
            big = matrix.astype(ml_dtypes.bfloat16)
            small = (matrix - big.astype(np.float64)).astype(ml_dtypes.bfloat16)
            nil = np.zeros_like(big)
            into = np.block([[big, small], [big, nil]])
            back = np.block([[big, big], [small, nil]])
            made.append((into, back))
        sets.append((made[0][0], made[1][1], made[1][0], made[0][1]))
    return [np.stack(each) for each in zip(*sets)]


def split(value):
    big = value.astype(BF16)
    return big, (value - big.astype(F32)).astype(BF16)


def march(source, target, beta, first, last, columns):
    levels = [{} for _ in range(STEPS + 1)]
    low, high, skew = -STEPS, RUN + STEPS, 1
    for front in range(low, high + STEPS * skew):
        for step in range(STEPS + 1):
            at = front - step * skew
            if step == 0:
                if at >= high:
                    continue
                value = source[pl.ds(PAD + at, 8, stride=RUN), :]
            else:
                if at - 1 < low + step - 1 or at + 1 >= high - step + 1:
                    continue
                before = levels[step - 1]
                value = (before[at - 1] + before[at + 1]) + beta * before[at]
                del before[at - 1]
            if step < STEPS:
                if at == -1:
                    value = jnp.where(first, 0.0, value)
                if at == columns - 7 * RUN:
                    value = jnp.where(last, 0.0, value)
            levels[step][at] = value
            if step == STEPS:
                target[pl.ds(at, 8, stride=RUN), :] = value


def kernel(
    tiles, groups, members, rows, columns,
    dif_ref, alpha_hbm, pert_hbm, inn_hbm, ow_hbm, w1f_hbm, w2f_hbm, w1a_hbm, w2a_hbm,
    out_hbm,
    alpha_v, pert_v, out_v, inn_v, ow_v, w1f, w2f, w1a, w2a,
    edge, edge_got, ph, lh, part, halo_part, got, halo_got, mine, other, mis, mis_halo,
    fs, gb, hb, gs, beta_v, scale_v,
    in_sem, w_sem, out_sem, ph_s, ph_r, rs_s, rs_r, rh_s, rh_r, x_s, x_r, ag_s, ag_r, ah_s, ah_r,
):
    fields = 2 * members
    g = lax.axis_index("grid")
    m = lax.axis_index("mem")
    quarters = groups // 2
    quarter, half = m // 2, lax.rem(m, 2)
    chunk_rows = rows // quarters
    variant = (g + tiles - 2) // (tiles - 1) + g // (tiles - 1)
    has_low, has_high = g > 0, g < tiles - 1

    loads = []
    for i in range(fields):
        level, member = i // members, i % members
        loads.append(pltpu.make_async_copy(pert_hbm.at[member, level], pert_v.at[i], in_sem.at[0, i]))
    for i in range(fields):
        level, member = i // members, i % members
        loads.append(pltpu.make_async_copy(alpha_hbm.at[member, level], alpha_v.at[i], in_sem.at[1, i]))
    weights = []
    for n, (src, dst) in enumerate(((w1f_hbm, w1f), (w2f_hbm, w2f), (w1a_hbm, w1a), (w2a_hbm, w2a))):
        weights.append(pltpu.make_async_copy(src.at[variant], dst, w_sem.at[n]))
    window = (slice(None), pl.ds(pl.multiple_of(quarter * chunk_rows, 8), chunk_rows))
    weights.append(pltpu.make_async_copy(inn_hbm.at[window], inn_v, w_sem.at[4]))
    weights.append(pltpu.make_async_copy(ow_hbm.at[window], ow_v, w_sem.at[5]))
    for copy in loads[:fields] + loads[fields : fields + 1] + weights[:4] + loads[fields + 1 :] + weights[4:]:
        copy.start()

    barrier = pltpu.get_barrier_semaphore()
    for k in range(1, quarters):
        pl.semaphore_signal(barrier, 1, device_id=(g, lax.rem(m + 2 * k, groups)), device_id_type=MESH)
    pl.semaphore_signal(barrier, 1, device_id=(g, m + 1 - 2 * half), device_id_type=MESH)

    @pl.when(has_low)
    def _():
        pl.semaphore_signal(barrier, 1, device_id=(g - 1, m), device_id_type=MESH)

    @pl.when(has_high)
    def _():
        pl.semaphore_signal(barrier, 1, device_id=(g + 1, m), device_id_type=MESH)

    part[...] = jnp.zeros_like(part)
    mode = lax.broadcasted_iota(jnp.int32, (8, BLOCK), 1) + 1
    cosine = jnp.cos(mode.astype(F32) * (np.pi / (BLOCK + 1)))
    for level in range(2):
        kx = jnp.full((8, BLOCK), dif_ref[0, level], F32)
        ky = jnp.full((8, BLOCK), dif_ref[1, level], F32)
        beta_v[level] = (1.0 - 2.0 * ky - 2.0 * kx + 2.0 * kx * cosine) / ky
        square = ky * ky
        fourth = square * square
        scale_v[level] = fourth * fourth * square
    gb[...] = jnp.zeros_like(gb)
    ph[...] = jnp.zeros_like(ph)

    @pl.when(g == 0)
    def _():
        mis_halo[:, 0] = jnp.zeros_like(mis_halo[:, 0])

    @pl.when(g == tiles - 1)
    def _():
        mis_halo[:, 1] = jnp.zeros_like(mis_halo[:, 1])

    for i in range(fields):
        loads[i].wait()
        level, at = i // members, STEPS * (i % members)
        edge[1, level, at : at + STEPS] = pert_v[i, 0:HALO, :].astype(F32)[:STEPS]
        edge[0, level, at : at + STEPS] = pert_v[i, rows - HALO : rows, :].astype(F32)[HALO - STEPS :]

    def edge_copy(level, side):
        return pltpu.make_async_remote_copy(
            src_ref=edge.at[side, level], dst_ref=edge_got.at[side, level],
            send_sem=ph_s.at[level, side], recv_sem=ph_r.at[level, side],
            device_id=(g + 1 - 2 * side, m), device_id_type=MESH,
        )

    def send_edges(level):
        @pl.when(has_high)
        def _():
            edge_copy(level, 0).start()

        @pl.when(has_low)
        def _():
            edge_copy(level, 1).start()

    def edges_sent(level):
        @pl.when(has_high)
        def _():
            edge_copy(level, 0).wait_send()

        @pl.when(has_low)
        def _():
            edge_copy(level, 1).wait_send()

    def start_exchange():
        neighbours = jnp.minimum(g, 1) + jnp.minimum(tiles - 1 - g, 1)
        pl.semaphore_wait(barrier, quarters + neighbours)
        send_edges(0)

    for copy in weights:
        copy.wait()

    def rs_copy(level, k):
        peer = lax.rem(quarter + k, quarters)
        return pltpu.make_async_remote_copy(
            src_ref=part.at[level, peer], dst_ref=got.at[level, quarter],
            send_sem=rs_s.at[level, k], recv_sem=rs_r.at[level, quarter],
            device_id=(g, 2 * peer + half), device_id_type=MESH,
        )

    def rh_copy(level, side):
        return pltpu.make_async_remote_copy(
            src_ref=halo_part.at[level, side], dst_ref=halo_got.at[level, quarter],
            send_sem=rh_s.at[level, side], recv_sem=rh_r.at[level, quarter],
            device_id=(g - 1 + 2 * side, 2 * (quarters - 1) * (1 - side) + half), device_id_type=MESH,
        )

    def pair_copy(level):
        return pltpu.make_async_remote_copy(
            src_ref=mine.at[level], dst_ref=other.at[level],
            send_sem=x_s.at[level], recv_sem=x_r.at[level],
            device_id=(g, m + 1 - 2 * half), device_id_type=MESH,
        )

    def ag_copy(level, k):
        peer = lax.rem(quarter + k, quarters)
        return pltpu.make_async_remote_copy(
            src_ref=mis.at[level, quarter], dst_ref=mis.at[level, quarter],
            send_sem=ag_s.at[level, k], recv_sem=ag_r.at[level, quarter],
            device_id=(g, 2 * peer + half), device_id_type=MESH,
        )

    def ah_copy(level, side):
        first = (chunk_rows - HALO) * (1 - side)
        return pltpu.make_async_remote_copy(
            src_ref=mis.at[level, (quarters - 1) * (1 - side), pl.ds(first, HALO)], dst_ref=mis_halo.at[level, side],
            send_sem=ah_s.at[level, side], recv_sem=ah_r.at[level, side],
            device_id=(g + 1 - 2 * side, m), device_id_type=MESH,
        )

    def landed(ref, sem):
        pltpu.make_async_copy(ref, ref, sem).wait()

    def send_sums(level):
        for k in range(1, quarters):
            rs_copy(level, k).start()

    def send_halo_sums(level):
        for side, there in ((0, has_low), (1, has_high)):

            @pl.when(there)
            def _():
                landed(edge_got.at[side, level], ph_r.at[level, side])
                for f in range(members):
                    value = edge_got[side, level, f * STEPS : (f + 1) * STEPS]
                    start = (HALO - STEPS) * (1 - side)
                    ph[side, level * members + f, start : start + STEPS] = value
                total = None
                for f in range(members):
                    i = level * members + f
                    term = lh[i, side] * ph[side, i]
                    total = term if total is None else total + term
                halo_part[level, side] = total
                rh_copy(level, side).start()

    at_low = (quarter == 0) & has_low
    at_high = (quarter == quarters - 1) & has_high

    def swap_sums(level):
        peers = [lax.rem(quarter + k, quarters) for k in range(1, quarters)]
        for p in peers:
            landed(got.at[level, p], rs_r.at[level, p])
        total = part[level, quarter]
        for p in peers:
            total = total + got[level, p]
        mine[level] = total
        for there, first in ((at_low, 0), (at_high, chunk_rows - HALO)):

            @pl.when(there)
            def _():
                for p in range(quarters):
                    landed(halo_got.at[level, p], rh_r.at[level, p])
                spot = slice(first, first + HALO)
                mine[level, spot] = mine[level, spot] + sum(halo_got[level, p] for p in range(quarters))

        pair_copy(level).start()

    def send_misfit(level):
        landed(other.at[level], x_r.at[level])
        scale = scale_v[level, 0:1, 0:1]
        mis[level, quarter] = ow_v[level] * ((mine[level] + other[level]) * scale - inn_v[level]) * scale
        for k in range(1, quarters):
            ag_copy(level, k).start()

    def take_misfit(level):
        for p in (0, quarters - 1):

            @pl.when(quarter != p)
            def _():
                landed(mis.at[level, p], ag_r.at[level, p])

            @pl.when(has_low if p == 0 else has_high)
            def _():
                ah_copy(level, 1 if p == 0 else 0).start()

        for p in range(1, quarters - 1):

            @pl.when(quarter != p)
            def _():
                landed(mis.at[level, p], ag_r.at[level, p])

    def take_halo(level):
        for side, there in ((0, has_low), (1, has_high)):

            @pl.when(there)
            def _():
                landed(mis_halo.at[level, side], ah_r.at[level, side])

    sub = lax.broadcasted_iota(jnp.int32, (8, BLOCK), 0)
    first, last = sub == 0, sub == 7
    wide = 256

    def to_modes(u, count, weight):
        for c in range(0, columns, wide):
            made = lax.dot_general(
                fs[u, 0:count, c : c + wide], weight[...], (((0,), (0,)), ((), ())), preferred_element_type=F32
            )
            gb[u, PAD + c : PAD + c + wide, :] = made[:, :BLOCK] + made[:, BLOCK:]

    def modes_out(u):
        for c in range(0, columns, 128):
            big, small = split(hb[u, c : c + 128, :])
            gs[u, c : c + 128, 0:BLOCK] = big
            gs[u, c : c + 128, BLOCK:] = small

    def from_modes(u, weight, c):
        return lax.dot_general(
            weight[...], gs[u, c : c + wide, :], (((1,), (1,)), ((), ())), preferred_element_type=F32
        )

    def forward(step, carry):
        level = step // (members // UNROLL)
        for u in range(UNROLL):
            i = step * UNROLL + u
            pltpu.make_async_copy(alpha_hbm.at[0, 0], alpha_v.at[i], in_sem.at[1, i]).wait()
            for c in range(0, columns, 128):
                big, small = split(alpha_v[i, :, c : c + 128])
                fs[u, 0:rows, c : c + 128] = big
                fs[u, rows : 2 * rows, c : c + 128] = small
        for u in range(UNROLL):
            to_modes(u, 2 * rows, w1f)
        for u in range(UNROLL):
            march(gb.at[u], hb.at[u], beta_v[level], first, last, columns)
            modes_out(u)
        for c in range(0, columns, wide):
            total = None
            for u in range(UNROLL):
                i = step * UNROLL + u
                made = from_modes(u, w2f, c)
                made = made[:BLOCK] + made[BLOCK:]
                lh[i, 0, :, c : c + wide] = made[rows : rows + HALO]
                lh[i, 1, :, c : c + wide] = made[rows + HALO :]
                term = made[:rows] * pert_v[i, :, c : c + wide].astype(F32)
                total = term if total is None else total + term
            for q in range(quarters):
                piece = total[q * chunk_rows : (q + 1) * chunk_rows]
                spot = (level, q, slice(None), slice(c, c + wide))
                part[spot] = piece if UNROLL == members else part[spot] + piece

        @pl.when(step == 0)
        def _():
            send_sums(0)
            edges_sent(0)
            send_edges(1)
            send_halo_sums(0)

        return carry

    start_exchange()
    lax.fori_loop(0, fields // UNROLL, forward, 0)
    send_sums(1)
    swap_sums(0)
    send_halo_sums(1)
    send_misfit(0)
    swap_sums(1)
    take_misfit(0)
    send_misfit(1)
    take_halo(0)

    def adjoint(step, carry):
        level = step // (members // UNROLL)

        @pl.when(step == members // UNROLL)
        def _():
            take_misfit(1)
            take_halo(1)

        for u in range(UNROLL):
            i = step * UNROLL + u
            for c in range(0, columns, 128):
                cut = slice(c, c + 128)
                ours = pert_v[i, :, cut].astype(F32)
                pieces = []
                for q in range(quarters):
                    pieces.append(ours[q * chunk_rows : (q + 1) * chunk_rows] * mis[level, q, :, cut])
                for side in range(2):
                    pieces.append(ph[side, i, :, cut] * mis_halo[level, side, :, cut])
                big, small = split(jnp.concatenate(pieces, axis=0))
                fs[u, 0:BLOCK, c : c + 128] = big
                fs[u, BLOCK : 2 * BLOCK, c : c + 128] = small
        for u in range(UNROLL):
            to_modes(u, 2 * BLOCK, w1a)
        for u in range(UNROLL):
            march(gb.at[u], hb.at[u], beta_v[level], first, last, columns)
            modes_out(u)
        for u in range(UNROLL):
            i = step * UNROLL + u
            for c in range(0, columns, wide):
                made = from_modes(u, w2a, c)
                out_v[i, :, c : c + wide] = alpha_v[i, :, c : c + wide] + (made[:rows] + made[rows:])
            pltpu.make_async_copy(out_v.at[i], out_hbm.at[i - level * members, level], out_sem.at[i]).start()
        return carry

    lax.fori_loop(0, fields // UNROLL, adjoint, 0)

    for i in range(fields):
        pltpu.make_async_copy(out_v.at[i], out_hbm.at[i % members, i // members], out_sem.at[i]).wait()
    edges_sent(1)
    for level in range(2):
        pair_copy(level).wait_send()
        for k in range(1, quarters):
            rs_copy(level, k).wait_send()
            ag_copy(level, k).wait_send()

        @pl.when(has_low)
        def _():
            rh_copy(level, 0).wait_send()
            ah_copy(level, 1).wait_send()

        @pl.when(has_high)
        def _():
            rh_copy(level, 1).wait_send()
            ah_copy(level, 0).wait_send()


def local(tiles, groups, alpha, perturbations, innovation, obs_weight, diffusivity):
    members, levels, rows, columns = alpha.shape
    fields = members * levels
    w1f, w2f, w1a, w2a = transforms(rows)
    any_space = pl.BlockSpec(memory_space=pltpu.HBM)
    dma = pltpu.SemaphoreType.DMA
    quarters = groups // 2
    chunk = (rows // quarters, columns)
    halo = (HALO, columns)
    packed = -(-STEPS * members // 8) * 8
    return pl.pallas_call(
        functools.partial(kernel, tiles, groups, members, rows, columns),
        out_shape=jax.ShapeDtypeStruct(alpha.shape, F32),
        in_specs=[pl.BlockSpec(memory_space=pltpu.SMEM)] + [any_space] * 8,
        out_specs=any_space,
        scratch_shapes=[
            pltpu.VMEM((fields, rows, columns), F32),
            pltpu.VMEM((fields, rows, columns), BF16),
            pltpu.VMEM((fields, rows, columns), F32),
            pltpu.VMEM((levels,) + chunk, F32),
            pltpu.VMEM((levels,) + chunk, F32),
            pltpu.VMEM(w1f.shape[1:], BF16),
            pltpu.VMEM(w2f.shape[1:], BF16),
            pltpu.VMEM(w1a.shape[1:], BF16),
            pltpu.VMEM(w2a.shape[1:], BF16),
            pltpu.VMEM((2, levels, packed, columns), F32),
            pltpu.VMEM((2, levels, packed, columns), F32),
            pltpu.VMEM((2, fields, HALO, columns), F32),
            pltpu.VMEM((fields, 2, HALO, columns), F32),
            pltpu.VMEM((levels, quarters) + chunk, F32),
            pltpu.VMEM((levels, 2) + halo, F32),
            pltpu.VMEM((levels, quarters) + chunk, F32),
            pltpu.VMEM((levels, quarters) + halo, F32),
            pltpu.VMEM((levels,) + chunk, F32),
            pltpu.VMEM((levels,) + chunk, F32),
            pltpu.VMEM((levels, quarters) + chunk, F32),
            pltpu.VMEM((levels, 2) + halo, F32),
            pltpu.VMEM((UNROLL, 2 * BLOCK, columns), BF16),
            pltpu.VMEM((UNROLL, PAD + 8 * RUN + PAD, BLOCK), F32),
            pltpu.VMEM((UNROLL, 8 * RUN, BLOCK), F32),
            pltpu.VMEM((UNROLL, 8 * RUN, 2 * BLOCK), BF16),
            pltpu.VMEM((levels, 8, BLOCK), F32),
            pltpu.VMEM((levels, 8, BLOCK), F32),
            dma((2, fields)),
            dma((6,)),
            dma((fields,)),
            dma((levels, 2)),
            dma((levels, 2)),
            dma((levels, quarters)),
            dma((levels, quarters)),
            dma((levels, 2)),
            dma((levels, quarters)),
            dma((levels,)),
            dma((levels,)),
            dma((levels, quarters)),
            dma((levels, quarters)),
            dma((levels, 2)),
            dma((levels, 2)),
        ],
        compiler_params=pltpu.CompilerParams(
            collective_id=0, has_side_effects=True, vmem_limit_bytes=60 * 2**20
        ),
    )(diffusivity, alpha, perturbations, innovation, obs_weight, w1f, w2f, w1a, w2a)


def solution(mesh):
    in_specs = (
        P("mem", None, "grid", None),
        P("mem", None, "grid", None),
        P(None, "grid", None),
        P(None, "grid", None),
        P(),
    )
    out_specs = P("mem", None, "grid", None)
    body = functools.partial(local, mesh.shape["grid"], mesh.shape["mem"])
    return jax.shard_map(body, mesh=mesh, in_specs=in_specs, out_specs=out_specs, check_vma=False)
```

```python
import functools

import jax
import jax.numpy as jnp
import ml_dtypes
import numpy as np
from jax import lax
from jax.experimental import pallas as pl
from jax.experimental.pallas import tpu as pltpu
from jax.sharding import PartitionSpec as P

STEPS = 10
UNROLL = 5
BLOCK = 128
HALO = 16
RUN = 97
PAD = 16
MESH = pl.DeviceIdType.MESH
F32 = jnp.float32
BF16 = jnp.bfloat16


def transforms(rows):
    index = np.arange(1, BLOCK + 1, dtype=np.float64)
    sine = np.sqrt(2.0 / (BLOCK + 1)) * np.sin(np.pi * np.outer(index, index) / (BLOCK + 1))
    none = np.zeros((HALO, BLOCK))
    sets = []
    for offset in (0, HALO, 2 * HALO):
        inner = sine[offset : offset + rows]
        low = sine[offset - HALO : offset] if offset else none
        high = sine[offset + rows : offset + rows + HALO] if offset < 2 * HALO else none
        wide = np.concatenate([inner, low, high])
        made = []
        for matrix in (inner, wide):
            big = matrix.astype(ml_dtypes.bfloat16)
            small = (matrix - big.astype(np.float64)).astype(ml_dtypes.bfloat16)
            nil = np.zeros_like(big)
            into = np.block([[big, small], [big, nil]])
            back = np.block([[big, big], [small, nil]])
            made.append((into, back))
        sets.append((made[0][0], made[1][1], made[1][0], made[0][1]))
    return [np.stack(each) for each in zip(*sets)]


def pack(ref, value):
    third = value.shape[1] // 3
    ref[0:STEPS] = value[:, : 2 * third]
    ref[STEPS : STEPS + STEPS // 2, :third] = value[: STEPS // 2, 2 * third :]
    ref[STEPS : STEPS + STEPS // 2, third:] = value[STEPS // 2 :, 2 * third :]


def unpack(block):
    third = block.shape[1] // 2
    tail = block[STEPS : STEPS + STEPS // 2]
    return jnp.concatenate([block[:STEPS], jnp.concatenate([tail[:, :third], tail[:, third:]], axis=0)], axis=1)


def split(value):
    big = value.astype(BF16)
    return big, (value - big.astype(F32)).astype(BF16)


def march(source, target, beta, first, last, columns):
    levels = [{} for _ in range(STEPS + 1)]
    low, high, skew = -STEPS, RUN + STEPS, 1
    for front in range(low, high + STEPS * skew):
        for step in range(STEPS + 1):
            at = front - step * skew
            if step == 0:
                if at >= high:
                    continue
                value = source[pl.ds(PAD + at, 8, stride=RUN), :]
            else:
                if at - 1 < low + step - 1 or at + 1 >= high - step + 1:
                    continue
                before = levels[step - 1]
                value = (before[at - 1] + before[at + 1]) + beta * before[at]
                del before[at - 1]
            if step < STEPS:
                if at == -1:
                    value = jnp.where(first, 0.0, value)
                if at == columns - 7 * RUN:
                    value = jnp.where(last, 0.0, value)
            levels[step][at] = value
            if step == STEPS:
                target[pl.ds(at, 8, stride=RUN), :] = value


def kernel(
    tiles, groups, members, rows, columns,
    dif_ref, alpha_hbm, pert_hbm, inn_hbm, ow_hbm, w1f_hbm, w2f_hbm, w1a_hbm, w2a_hbm,
    out_hbm,
    alpha_v, pert_v, out_v, inn_v, ow_v, w1f, w2f, w1a, w2a,
    edge, edge_got, ph, lh, part, halo_part, got, halo_got, mine, other, mis, mis_halo, mis_edge, mis_got,
    fs, gb, hb, gs, beta_v, scale_v,
    in_sem, w_sem, out_sem, ph_s, ph_r, rs_s, rs_r, rh_s, rh_r, x_s, x_r, ag_s, ag_r, ah_s, ah_r,
):
    fields = 2 * members
    g = lax.axis_index("grid")
    m = lax.axis_index("mem")
    quarters = groups // 2
    quarter, half = m // 2, lax.rem(m, 2)
    chunk_rows = rows // quarters
    variant = (g + tiles - 2) // (tiles - 1) + g // (tiles - 1)
    has_low, has_high = g > 0, g < tiles - 1

    loads = []
    for i in range(fields):
        level, member = i // members, i % members
        loads.append(pltpu.make_async_copy(pert_hbm.at[member, level], pert_v.at[i], in_sem.at[0, i]))
    for i in range(fields):
        level, member = i // members, i % members
        loads.append(pltpu.make_async_copy(alpha_hbm.at[member, level], alpha_v.at[i], in_sem.at[1, i]))
    weights = []
    for n, (src, dst) in enumerate(((w1f_hbm, w1f), (w2f_hbm, w2f), (w1a_hbm, w1a), (w2a_hbm, w2a))):
        weights.append(pltpu.make_async_copy(src.at[variant], dst, w_sem.at[n]))
    window = (slice(None), pl.ds(pl.multiple_of(quarter * chunk_rows, 8), chunk_rows))
    weights.append(pltpu.make_async_copy(inn_hbm.at[window], inn_v, w_sem.at[4]))
    weights.append(pltpu.make_async_copy(ow_hbm.at[window], ow_v, w_sem.at[5]))
    for copy in loads[:fields] + loads[fields : fields + 1] + weights[:4] + loads[fields + 1 :] + weights[4:]:
        copy.start()

    barrier = pltpu.get_barrier_semaphore()
    for k in range(1, quarters):
        pl.semaphore_signal(barrier, 1, device_id=(g, lax.rem(m + 2 * k, groups)), device_id_type=MESH)
    pl.semaphore_signal(barrier, 1, device_id=(g, m + 1 - 2 * half), device_id_type=MESH)

    @pl.when(has_low)
    def _():
        pl.semaphore_signal(barrier, 1, device_id=(g - 1, m), device_id_type=MESH)

    @pl.when(has_high)
    def _():
        pl.semaphore_signal(barrier, 1, device_id=(g + 1, m), device_id_type=MESH)

    part[...] = jnp.zeros_like(part)
    mode = lax.broadcasted_iota(jnp.int32, (8, BLOCK), 1) + 1
    cosine = jnp.cos(mode.astype(F32) * (np.pi / (BLOCK + 1)))
    for level in range(2):
        kx = jnp.full((8, BLOCK), dif_ref[0, level], F32)
        ky = jnp.full((8, BLOCK), dif_ref[1, level], F32)
        beta_v[level] = (1.0 - 2.0 * ky - 2.0 * kx + 2.0 * kx * cosine) / ky
        square = ky * ky
        fourth = square * square
        scale_v[level] = fourth * fourth * square
    gb[...] = jnp.zeros_like(gb)
    ph[...] = jnp.zeros_like(ph)

    mis_halo[...] = jnp.zeros_like(mis_halo)
    halo_part[...] = jnp.zeros_like(halo_part)
    mis_edge[...] = jnp.zeros_like(mis_edge)

    for i in range(fields):
        loads[i].wait()
        level, at = i // members, STEPS * (i % members)
        edge[1, level, at : at + STEPS] = pert_v[i, 0:HALO, :].astype(F32)[:STEPS]
        edge[0, level, at : at + STEPS] = pert_v[i, rows - HALO : rows, :].astype(F32)[HALO - STEPS :]

    def edge_copy(level, side):
        return pltpu.make_async_remote_copy(
            src_ref=edge.at[side, level], dst_ref=edge_got.at[side, level],
            send_sem=ph_s.at[level, side], recv_sem=ph_r.at[level, side],
            device_id=(g + 1 - 2 * side, m), device_id_type=MESH,
        )

    def send_edges(level):
        @pl.when(has_high)
        def _():
            edge_copy(level, 0).start()

        @pl.when(has_low)
        def _():
            edge_copy(level, 1).start()

    def edges_sent(level):
        @pl.when(has_high)
        def _():
            edge_copy(level, 0).wait_send()

        @pl.when(has_low)
        def _():
            edge_copy(level, 1).wait_send()

    def start_exchange():
        neighbours = jnp.minimum(g, 1) + jnp.minimum(tiles - 1 - g, 1)
        pl.semaphore_wait(barrier, quarters + neighbours)
        send_edges(0)
        send_edges(1)

    for copy in weights:
        copy.wait()

    def rs_copy(level, k):
        peer = lax.rem(quarter + k, quarters)
        return pltpu.make_async_remote_copy(
            src_ref=part.at[level, peer], dst_ref=got.at[level, quarter],
            send_sem=rs_s.at[level, k], recv_sem=rs_r.at[level, quarter],
            device_id=(g, 2 * peer + half), device_id_type=MESH,
        )

    def rh_copy(level, side):
        return pltpu.make_async_remote_copy(
            src_ref=halo_part.at[level, side], dst_ref=halo_got.at[level, quarter],
            send_sem=rh_s.at[level, side], recv_sem=rh_r.at[level, quarter],
            device_id=(g - 1 + 2 * side, 2 * (quarters - 1) * (1 - side) + half), device_id_type=MESH,
        )

    def pair_copy(level):
        return pltpu.make_async_remote_copy(
            src_ref=mine.at[level], dst_ref=other.at[level],
            send_sem=x_s.at[level], recv_sem=x_r.at[level],
            device_id=(g, m + 1 - 2 * half), device_id_type=MESH,
        )

    def ag_copy(level, k):
        peer = lax.rem(quarter + k, quarters)
        return pltpu.make_async_remote_copy(
            src_ref=mis.at[level, quarter], dst_ref=mis.at[level, quarter],
            send_sem=ag_s.at[level, k], recv_sem=ag_r.at[level, quarter],
            device_id=(g, 2 * peer + half), device_id_type=MESH,
        )

    def ah_copy(level, side, p):
        return pltpu.make_async_remote_copy(
            src_ref=mis_edge.at[level, side], dst_ref=mis_got.at[level, side],
            send_sem=ah_s.at[level, side, p], recv_sem=ah_r.at[level, side],
            device_id=(g + 1 - 2 * side, 2 * p + half), device_id_type=MESH,
        )

    def landed(ref, sem):
        pltpu.make_async_copy(ref, ref, sem).wait()

    def send_sums(level):
        for k in range(1, quarters):
            rs_copy(level, k).start()

    def send_halo_sums(level):
        for side, there in ((0, has_low), (1, has_high)):

            @pl.when(there)
            def _():
                landed(edge_got.at[side, level], ph_r.at[level, side])
                for f in range(members):
                    value = edge_got[side, level, f * STEPS : (f + 1) * STEPS]
                    start = (HALO - STEPS) * (1 - side)
                    ph[side, level * members + f, start : start + STEPS] = value
                total = None
                for f in range(members):
                    i = level * members + f
                    term = lh[i, side] * ph[side, i]
                    total = term if total is None else total + term
                inner = (HALO - STEPS) * (1 - side)
                pack(halo_part.at[level, side], total[inner : inner + STEPS])
                rh_copy(level, side).start()

    at_low = (quarter == 0) & has_low
    at_high = (quarter == quarters - 1) & has_high

    def swap_sums(level):
        peers = [lax.rem(quarter + k, quarters) for k in range(1, quarters)]
        for p in peers:
            landed(got.at[level, p], rs_r.at[level, p])
        total = part[level, quarter]
        for p in peers:
            total = total + got[level, p]
        mine[level] = total
        for there, begin in ((at_low, 0), (at_high, chunk_rows - STEPS)):

            @pl.when(there)
            def _():
                for p in range(quarters):
                    landed(halo_got.at[level, p], rh_r.at[level, p])
                spot = slice(begin, begin + STEPS)
                mine[level, spot] = mine[level, spot] + unpack(sum(halo_got[level, p] for p in range(quarters)))

        pair_copy(level).start()

    def send_misfit(level):
        landed(other.at[level], x_r.at[level])
        scale = scale_v[level, 0:1, 0:1]
        mis[level, quarter] = ow_v[level] * ((mine[level] + other[level]) * scale - inn_v[level]) * scale
        for k in range(1, quarters):
            ag_copy(level, k).start()
        for there, side, begin in ((at_low, 1, 0), (at_high, 0, chunk_rows - STEPS)):

            @pl.when(there)
            def _():
                pack(mis_edge.at[level, side], mis[level, quarter, begin : begin + STEPS])
                for p in range(quarters):
                    ah_copy(level, side, p).start()

    def take_misfit(level):
        for k in range(1, quarters):
            p = lax.rem(quarter + k, quarters)
            landed(mis.at[level, p], ag_r.at[level, p])

    def take_halo(level):
        for side, there in ((0, has_low), (1, has_high)):

            @pl.when(there)
            def _():
                landed(mis_got.at[level, side], ah_r.at[level, side])
                inner = (HALO - STEPS) * (1 - side)
                mis_halo[level, side, inner : inner + STEPS] = unpack(mis_got[level, side])

    sub = lax.broadcasted_iota(jnp.int32, (8, BLOCK), 0)
    first, last = sub == 0, sub == 7
    wide = 256

    def to_modes(u, count, weight):
        for c in range(0, columns, wide):
            made = lax.dot_general(
                fs[u, 0:count, c : c + wide], weight[...], (((0,), (0,)), ((), ())), preferred_element_type=F32
            )
            gb[u, PAD + c : PAD + c + wide, :] = made[:, :BLOCK] + made[:, BLOCK:]

    def modes_out(u):
        for c in range(0, columns, 128):
            big, small = split(hb[u, c : c + 128, :])
            gs[u, c : c + 128, 0:BLOCK] = big
            gs[u, c : c + 128, BLOCK:] = small

    def from_modes(u, weight, c):
        return lax.dot_general(
            weight[...], gs[u, c : c + wide, :], (((1,), (1,)), ((), ())), preferred_element_type=F32
        )

    def forward(level, begin, count):
        batch = [(u, level * members + begin + u) for u in range(count)]
        for u, i in batch:
            loads[fields + i].wait()
            for c in range(0, columns, 128):
                big, small = split(alpha_v[i, :, c : c + 128])
                fs[u, 0:rows, c : c + 128] = big
                fs[u, rows : 2 * rows, c : c + 128] = small
        for u, i in batch:
            to_modes(u, 2 * rows, w1f)
        for u, i in batch:
            march(gb.at[u], hb.at[u], beta_v[level], first, last, columns)
            modes_out(u)
        for c in range(0, columns, wide):
            total = None
            for u, i in batch:
                made = from_modes(u, w2f, c)
                made = made[:BLOCK] + made[BLOCK:]
                lh[i, 0, :, c : c + wide] = made[rows : rows + HALO]
                lh[i, 1, :, c : c + wide] = made[rows + HALO :]
                term = made[:rows] * pert_v[i, :, c : c + wide].astype(F32)
                total = term if total is None else total + term
            for q in range(quarters):
                piece = total[q * chunk_rows : (q + 1) * chunk_rows]
                spot = (level, q, slice(None), slice(c, c + wide))
                part[spot] = piece if begin == 0 else part[spot] + piece

    def adjoint(level, carry):
        @pl.when(level == 1)
        def _():
            take_misfit(1)
            take_halo(1)

        batch = [(u, level * members + u) for u in range(members)]
        for u, i in batch:
            for c in range(0, columns, 128):
                cut = slice(c, c + 128)
                ours = pert_v[i, :, cut].astype(F32)
                pieces = []
                for q in range(quarters):
                    pieces.append(ours[q * chunk_rows : (q + 1) * chunk_rows] * mis[level, q, :, cut])
                for side in range(2):
                    pieces.append(ph[side, i, :, cut] * mis_halo[level, side, :, cut])
                big, small = split(jnp.concatenate(pieces, axis=0))
                fs[u, 0:BLOCK, c : c + 128] = big
                fs[u, BLOCK : 2 * BLOCK, c : c + 128] = small
        for u, i in batch:
            to_modes(u, 2 * BLOCK, w1a)
        for u, i in batch:
            march(gb.at[u], hb.at[u], beta_v[level], first, last, columns)
            modes_out(u)
        for u, i in batch:
            for c in range(0, columns, wide):
                made = from_modes(u, w2a, c)
                out_v[i, :, c : c + wide] = alpha_v[i, :, c : c + wide] + (made[:rows] + made[rows:])
            pltpu.make_async_copy(out_v.at[i], out_hbm.at[u, level], out_sem.at[i]).start()
        return carry

    start_exchange()
    forward(0, 0, members)
    send_sums(0)
    forward(1, 0, 2)
    send_halo_sums(0)
    forward(1, 2, members - 2)
    send_sums(1)
    send_halo_sums(1)
    swap_sums(0)
    send_misfit(0)
    swap_sums(1)
    send_misfit(1)
    take_misfit(0)
    take_halo(0)
    lax.fori_loop(0, 2, adjoint, 0)

    for i in range(fields):
        pltpu.make_async_copy(out_v.at[i], out_hbm.at[i % members, i // members], out_sem.at[i]).wait()
    for level in range(2):
        edges_sent(level)
        pair_copy(level).wait_send()
        for k in range(1, quarters):
            rs_copy(level, k).wait_send()
            ag_copy(level, k).wait_send()

        @pl.when(has_low)
        def _():
            rh_copy(level, 0).wait_send()

        @pl.when(has_high)
        def _():
            rh_copy(level, 1).wait_send()

        for there, side in ((at_low, 1), (at_high, 0)):

            @pl.when(there)
            def _():
                for p in range(quarters):
                    ah_copy(level, side, p).wait_send()


def local(tiles, groups, alpha, perturbations, innovation, obs_weight, diffusivity):
    members, levels, rows, columns = alpha.shape
    fields = members * levels
    w1f, w2f, w1a, w2a = transforms(rows)
    any_space = pl.BlockSpec(memory_space=pltpu.HBM)
    dma = pltpu.SemaphoreType.DMA
    quarters = groups // 2
    chunk = (rows // quarters, columns)
    halo = (HALO, columns)
    dense = (HALO, columns // 3 * 2)
    packed = -(-STEPS * members // 8) * 8
    made = pl.pallas_call(
        functools.partial(kernel, tiles, groups, members, rows, columns),
        out_shape=jax.ShapeDtypeStruct(alpha.shape, F32),
        in_specs=[pl.BlockSpec(memory_space=pltpu.SMEM)] + [any_space] * 8,
        out_specs=any_space,
        scratch_shapes=[
            pltpu.VMEM((fields, rows, columns), F32),
            pltpu.VMEM((fields, rows, columns), BF16),
            pltpu.VMEM((fields, rows, columns), F32),
            pltpu.VMEM((levels,) + chunk, F32),
            pltpu.VMEM((levels,) + chunk, F32),
            pltpu.VMEM(w1f.shape[1:], BF16),
            pltpu.VMEM(w2f.shape[1:], BF16),
            pltpu.VMEM(w1a.shape[1:], BF16),
            pltpu.VMEM(w2a.shape[1:], BF16),
            pltpu.VMEM((2, levels, packed, columns), F32),
            pltpu.VMEM((2, levels, packed, columns), F32),
            pltpu.VMEM((2, fields, HALO, columns), F32),
            pltpu.VMEM((fields, 2, HALO, columns), F32),
            pltpu.VMEM((levels, quarters) + chunk, F32),
            pltpu.VMEM((levels, 2) + dense, F32),
            pltpu.VMEM((levels, quarters) + chunk, F32),
            pltpu.VMEM((levels, quarters) + dense, F32),
            pltpu.VMEM((levels,) + chunk, F32),
            pltpu.VMEM((levels,) + chunk, F32),
            pltpu.VMEM((levels, quarters) + chunk, F32),
            pltpu.VMEM((levels, 2) + halo, F32),
            pltpu.VMEM((levels, 2) + dense, F32),
            pltpu.VMEM((levels, 2) + dense, F32),
            pltpu.VMEM((UNROLL, 2 * BLOCK, columns), BF16),
            pltpu.VMEM((UNROLL, PAD + 8 * RUN + PAD, BLOCK), F32),
            pltpu.VMEM((UNROLL, 8 * RUN, BLOCK), F32),
            pltpu.VMEM((UNROLL, 8 * RUN, 2 * BLOCK), BF16),
            pltpu.VMEM((levels, 8, BLOCK), F32),
            pltpu.VMEM((levels, 8, BLOCK), F32),
            dma((2, fields)),
            dma((6,)),
            dma((fields,)),
            dma((levels, 2)),
            dma((levels, 2)),
            dma((levels, quarters)),
            dma((levels, quarters)),
            dma((levels, 2)),
            dma((levels, quarters)),
            dma((levels,)),
            dma((levels,)),
            dma((levels, quarters)),
            dma((levels, quarters)),
            dma((levels, 2, quarters)),
            dma((levels, 2)),
        ],
        compiler_params=pltpu.CompilerParams(
            collective_id=0, has_side_effects=True, vmem_limit_bytes=60 * 2**20
        ),
    )(diffusivity, alpha, perturbations, innovation, obs_weight, w1f, w2f, w1a, w2a)
    return pl.pallas_call(
        pass_on,
        out_shape=jax.ShapeDtypeStruct(alpha.shape, F32),
        in_specs=[any_space],
        out_specs=any_space,
        scratch_shapes=[pltpu.VMEM(alpha.shape, F32), dma((2, fields))],
        compiler_params=pltpu.CompilerParams(vmem_limit_bytes=60 * 2**20),
    )(made)


def pass_on(src, dst, held, sem):
    fields = [(i, j) for i in range(src.shape[0]) for j in range(src.shape[1])]
    reads = [pltpu.make_async_copy(src.at[f], held.at[f], sem.at[0, n]) for n, f in enumerate(fields)]
    writes = [pltpu.make_async_copy(held.at[f], dst.at[f], sem.at[1, n]) for n, f in enumerate(fields)]
    for copy in reads:
        copy.start()
    for read, write in zip(reads, writes):
        read.wait()
        write.start()
    for copy in writes:
        copy.wait()


def solution(mesh):
    in_specs = (
        P("mem", None, "grid", None),
        P("mem", None, "grid", None),
        P(None, "grid", None),
        P(None, "grid", None),
        P(),
    )
    out_specs = P("mem", None, "grid", None)
    body = functools.partial(local, mesh.shape["grid"], mesh.shape["mem"])
    return jax.shard_map(body, mesh=mesh, in_specs=in_specs, out_specs=out_specs, check_vma=False)
```

```python
import functools

import jax
import jax.numpy as jnp
import ml_dtypes
import numpy as np
from jax import lax
from jax.experimental import pallas as pl
from jax.experimental.pallas import tpu as pltpu
from jax.sharding import PartitionSpec as P

STEPS = 10
UNROLL = 5
BLOCK = 128
HALO = 16
RUN = 97
PAD = 16
MESH = pl.DeviceIdType.MESH
F32 = jnp.float32
BF16 = jnp.bfloat16


def transforms(rows):
    index = np.arange(1, BLOCK + 1, dtype=np.float64)
    sine = np.sqrt(2.0 / (BLOCK + 1)) * np.sin(np.pi * np.outer(index, index) / (BLOCK + 1))
    none = np.zeros((HALO, BLOCK))
    sets = []
    for offset in (0, HALO, 2 * HALO):
        inner = sine[offset : offset + rows]
        low = sine[offset - HALO : offset] if offset else none
        high = sine[offset + rows : offset + rows + HALO] if offset < 2 * HALO else none
        wide = np.concatenate([inner, low, high])
        made = []
        for matrix in (inner, wide):
            big = matrix.astype(ml_dtypes.bfloat16)
            small = (matrix - big.astype(np.float64)).astype(ml_dtypes.bfloat16)
            nil = np.zeros_like(big)
            into = np.block([[big, small], [big, nil]])
            back = np.block([[big, big], [small, nil]])
            made.append((into, back))
        sets.append((made[0][0], made[1][1], made[1][0], made[0][1]))
    return [np.stack(each) for each in zip(*sets)]


def pack(ref, value):
    third = value.shape[1] // 3
    ref[0:STEPS] = value[:, : 2 * third]
    ref[STEPS : STEPS + STEPS // 2, :third] = value[: STEPS // 2, 2 * third :]
    ref[STEPS : STEPS + STEPS // 2, third:] = value[STEPS // 2 :, 2 * third :]


def unpack(block):
    third = block.shape[1] // 2
    tail = block[STEPS : STEPS + STEPS // 2]
    return jnp.concatenate([block[:STEPS], jnp.concatenate([tail[:, :third], tail[:, third:]], axis=0)], axis=1)


def split(value):
    big = value.astype(BF16)
    return big, (value - big.astype(F32)).astype(BF16)


def march(source, target, beta, first, last, columns):
    levels = [{} for _ in range(STEPS + 1)]
    low, high, skew = -STEPS, RUN + STEPS, 1
    for front in range(low, high + STEPS * skew):
        for step in range(STEPS + 1):
            at = front - step * skew
            if step == 0:
                if at >= high:
                    continue
                value = source[pl.ds(PAD + at, 8, stride=RUN), :]
            else:
                if at - 1 < low + step - 1 or at + 1 >= high - step + 1:
                    continue
                before = levels[step - 1]
                value = (before[at - 1] + before[at + 1]) + beta * before[at]
                del before[at - 1]
            if step < STEPS:
                if at == -1:
                    value = jnp.where(first, 0.0, value)
                if at == columns - 7 * RUN:
                    value = jnp.where(last, 0.0, value)
            levels[step][at] = value
            if step == STEPS:
                target[pl.ds(at, 8, stride=RUN), :] = value


def kernel(
    tiles, groups, members, rows, columns,
    dif_ref, alpha_hbm, pert_hbm, inn_hbm, ow_hbm, w1f_hbm, w2f_hbm, w1a_hbm, w2a_hbm,
    out_hbm,
    alpha_v, pert_v, out_v, inn_v, ow_v, w1f, w2f, w1a, w2a,
    edge, edge_got, ph, lh, part, halo_part, got, halo_got, mine, other, mis, mis_halo, mis_edge, mis_got,
    fs, gb, hb, gs, beta_v, scale_v,
    in_sem, w_sem, out_sem, ph_s, ph_r, rs_s, rs_r, rh_s, rh_r, x_s, x_r, ag_s, ag_r, ah_s, ah_r,
):
    fields = 2 * members
    g = lax.axis_index("grid")
    m = lax.axis_index("mem")
    quarters = groups // 2
    quarter, half = m // 2, lax.rem(m, 2)
    chunk_rows = rows // quarters
    variant = (g + tiles - 2) // (tiles - 1) + g // (tiles - 1)
    has_low, has_high = g > 0, g < tiles - 1

    loads = []
    for i in range(fields):
        level, member = i // members, i % members
        loads.append(pltpu.make_async_copy(pert_hbm.at[member, level], pert_v.at[i], in_sem.at[0, i]))
    for i in range(fields):
        level, member = i // members, i % members
        loads.append(pltpu.make_async_copy(alpha_hbm.at[member, level], alpha_v.at[i], in_sem.at[1, i]))
    weights = []
    for n, (src, dst) in enumerate(((w1f_hbm, w1f), (w2f_hbm, w2f), (w1a_hbm, w1a), (w2a_hbm, w2a))):
        weights.append(pltpu.make_async_copy(src.at[variant], dst, w_sem.at[n]))
    window = (slice(None), pl.ds(pl.multiple_of(quarter * chunk_rows, 8), chunk_rows))
    weights.append(pltpu.make_async_copy(inn_hbm.at[window], inn_v, w_sem.at[4]))
    weights.append(pltpu.make_async_copy(ow_hbm.at[window], ow_v, w_sem.at[5]))
    for copy in loads[:fields] + loads[fields : fields + 1] + weights[:4] + loads[fields + 1 :] + weights[4:]:
        copy.start()

    barrier = pltpu.get_barrier_semaphore()
    for k in range(1, quarters):
        pl.semaphore_signal(barrier, 1, device_id=(g, lax.rem(m + 2 * k, groups)), device_id_type=MESH)
    pl.semaphore_signal(barrier, 1, device_id=(g, m + 1 - 2 * half), device_id_type=MESH)

    @pl.when(has_low)
    def _():
        pl.semaphore_signal(barrier, 1, device_id=(g - 1, m), device_id_type=MESH)

    @pl.when(has_high)
    def _():
        pl.semaphore_signal(barrier, 1, device_id=(g + 1, m), device_id_type=MESH)

    part[...] = jnp.zeros_like(part)
    mode = lax.broadcasted_iota(jnp.int32, (8, BLOCK), 1) + 1
    cosine = jnp.cos(mode.astype(F32) * (np.pi / (BLOCK + 1)))
    for level in range(2):
        kx = jnp.full((8, BLOCK), dif_ref[0, level], F32)
        ky = jnp.full((8, BLOCK), dif_ref[1, level], F32)
        beta_v[level] = (1.0 - 2.0 * ky - 2.0 * kx + 2.0 * kx * cosine) / ky
        square = ky * ky
        fourth = square * square
        scale_v[level] = fourth * fourth * square
    gb[...] = jnp.zeros_like(gb)
    ph[...] = jnp.zeros_like(ph)

    mis_halo[...] = jnp.zeros_like(mis_halo)
    halo_part[...] = jnp.zeros_like(halo_part)
    mis_edge[...] = jnp.zeros_like(mis_edge)

    for i in range(fields):
        loads[i].wait()
        level, at = i // members, STEPS * (i % members)
        edge[1, level, at : at + STEPS] = pert_v[i, 0:HALO, :].astype(F32)[:STEPS]
        edge[0, level, at : at + STEPS] = pert_v[i, rows - HALO : rows, :].astype(F32)[HALO - STEPS :]

    def edge_copy(level, side):
        return pltpu.make_async_remote_copy(
            src_ref=edge.at[side, level], dst_ref=edge_got.at[side, level],
            send_sem=ph_s.at[level, side], recv_sem=ph_r.at[level, side],
            device_id=(g + 1 - 2 * side, m), device_id_type=MESH,
        )

    def send_edges(level):
        @pl.when(has_high)
        def _():
            edge_copy(level, 0).start()

        @pl.when(has_low)
        def _():
            edge_copy(level, 1).start()

    def edges_sent(level):
        @pl.when(has_high)
        def _():
            edge_copy(level, 0).wait_send()

        @pl.when(has_low)
        def _():
            edge_copy(level, 1).wait_send()

    def start_exchange():
        neighbours = jnp.minimum(g, 1) + jnp.minimum(tiles - 1 - g, 1)
        pl.semaphore_wait(barrier, quarters + neighbours)
        send_edges(0)

    for copy in weights:
        copy.wait()

    def rs_copy(level, k):
        peer = lax.rem(quarter + k, quarters)
        return pltpu.make_async_remote_copy(
            src_ref=part.at[level, peer], dst_ref=got.at[level, quarter],
            send_sem=rs_s.at[level, k], recv_sem=rs_r.at[level, quarter],
            device_id=(g, 2 * peer + half), device_id_type=MESH,
        )

    def rh_copy(level, side):
        return pltpu.make_async_remote_copy(
            src_ref=halo_part.at[level, side], dst_ref=halo_got.at[level, quarter],
            send_sem=rh_s.at[level, side], recv_sem=rh_r.at[level, quarter],
            device_id=(g - 1 + 2 * side, 2 * (quarters - 1) * (1 - side) + half), device_id_type=MESH,
        )

    def pair_copy(level):
        return pltpu.make_async_remote_copy(
            src_ref=mine.at[level], dst_ref=other.at[level],
            send_sem=x_s.at[level], recv_sem=x_r.at[level],
            device_id=(g, m + 1 - 2 * half), device_id_type=MESH,
        )

    def ag_copy(level, k):
        peer = lax.rem(quarter + k, quarters)
        return pltpu.make_async_remote_copy(
            src_ref=mis.at[level, quarter], dst_ref=mis.at[level, quarter],
            send_sem=ag_s.at[level, k], recv_sem=ag_r.at[level, quarter],
            device_id=(g, 2 * peer + half), device_id_type=MESH,
        )

    def ah_copy(level, side, p):
        return pltpu.make_async_remote_copy(
            src_ref=mis_edge.at[level, side], dst_ref=mis_got.at[level, side],
            send_sem=ah_s.at[level, side, p], recv_sem=ah_r.at[level, side],
            device_id=(g + 1 - 2 * side, 2 * p + half), device_id_type=MESH,
        )

    def landed(ref, sem):
        pltpu.make_async_copy(ref, ref, sem).wait()

    def send_sums(level):
        for k in range(1, quarters):
            rs_copy(level, k).start()

    def send_halo_sums(level):
        for side, there in ((0, has_low), (1, has_high)):

            @pl.when(there)
            def _():
                landed(edge_got.at[side, level], ph_r.at[level, side])
                for f in range(members):
                    value = edge_got[side, level, f * STEPS : (f + 1) * STEPS]
                    start = (HALO - STEPS) * (1 - side)
                    ph[side, level * members + f, start : start + STEPS] = value
                total = None
                for f in range(members):
                    i = level * members + f
                    term = lh[i, side] * ph[side, i]
                    total = term if total is None else total + term
                inner = (HALO - STEPS) * (1 - side)
                pack(halo_part.at[level, side], total[inner : inner + STEPS])
                rh_copy(level, side).start()

    at_low = (quarter == 0) & has_low
    at_high = (quarter == quarters - 1) & has_high

    def swap_sums(level):
        peers = [lax.rem(quarter + k, quarters) for k in range(1, quarters)]
        for p in peers:
            landed(got.at[level, p], rs_r.at[level, p])
        total = part[level, quarter]
        for p in peers:
            total = total + got[level, p]
        mine[level] = total
        for there, begin in ((at_low, 0), (at_high, chunk_rows - STEPS)):

            @pl.when(there)
            def _():
                for p in range(quarters):
                    landed(halo_got.at[level, p], rh_r.at[level, p])
                spot = slice(begin, begin + STEPS)
                mine[level, spot] = mine[level, spot] + unpack(sum(halo_got[level, p] for p in range(quarters)))

        pair_copy(level).start()

    def send_misfit(level):
        landed(other.at[level], x_r.at[level])
        scale = scale_v[level, 0:1, 0:1]
        mis[level, quarter] = ow_v[level] * ((mine[level] + other[level]) * scale - inn_v[level]) * scale
        for there, side, begin in ((at_low, 1, 0), (at_high, 0, chunk_rows - STEPS)):

            @pl.when(there)
            def _():
                pack(mis_edge.at[level, side], mis[level, quarter, begin : begin + STEPS])
                for p in range(quarters):
                    ah_copy(level, side, p).start()

        for k in range(1, quarters):
            ag_copy(level, k).start()

    def take_misfit(level):
        for k in range(1, quarters):
            p = lax.rem(quarter + k, quarters)
            landed(mis.at[level, p], ag_r.at[level, p])

    def take_halo(level):
        for side, there in ((0, has_low), (1, has_high)):

            @pl.when(there)
            def _():
                landed(mis_got.at[level, side], ah_r.at[level, side])
                inner = (HALO - STEPS) * (1 - side)
                mis_halo[level, side, inner : inner + STEPS] = unpack(mis_got[level, side])

    sub = lax.broadcasted_iota(jnp.int32, (8, BLOCK), 0)
    first, last = sub == 0, sub == 7
    wide = 256

    def to_modes(u, count, weight):
        for c in range(0, columns, wide):
            made = lax.dot_general(
                fs[u, 0:count, c : c + wide], weight[...], (((0,), (0,)), ((), ())), preferred_element_type=F32
            )
            gb[u, PAD + c : PAD + c + wide, :] = made[:, :BLOCK] + made[:, BLOCK:]

    def modes_out(u):
        for c in range(0, columns, 128):
            big, small = split(hb[u, c : c + 128, :])
            gs[u, c : c + 128, 0:BLOCK] = big
            gs[u, c : c + 128, BLOCK:] = small

    def from_modes(u, weight, c):
        return lax.dot_general(
            weight[...], gs[u, c : c + wide, :], (((1,), (1,)), ((), ())), preferred_element_type=F32
        )

    def forward(level, begin, count):
        batch = [(u, level * members + begin + u) for u in range(count)]
        for u, i in batch:
            loads[fields + i].wait()
            for c in range(0, columns, 128):
                big, small = split(alpha_v[i, :, c : c + 128])
                fs[u, 0:rows, c : c + 128] = big
                fs[u, rows : 2 * rows, c : c + 128] = small
        for u, i in batch:
            to_modes(u, 2 * rows, w1f)
        for u, i in batch:
            march(gb.at[u], hb.at[u], beta_v[level], first, last, columns)
            modes_out(u)
        for c in range(0, columns, wide):
            total = None
            for u, i in batch:
                made = from_modes(u, w2f, c)
                made = made[:BLOCK] + made[BLOCK:]
                lh[i, 0, :, c : c + wide] = made[rows : rows + HALO]
                lh[i, 1, :, c : c + wide] = made[rows + HALO :]
                term = made[:rows] * pert_v[i, :, c : c + wide].astype(F32)
                total = term if total is None else total + term
            for q in range(quarters):
                piece = total[q * chunk_rows : (q + 1) * chunk_rows]
                spot = (level, q, slice(None), slice(c, c + wide))
                part[spot] = piece if begin == 0 else part[spot] + piece

    def adjoint(level, carry):
        @pl.when(level == 1)
        def _():
            take_misfit(1)
            take_halo(1)

        batch = [(u, level * members + u) for u in range(members)]
        for u, i in batch:
            for c in range(0, columns, 128):
                cut = slice(c, c + 128)
                ours = pert_v[i, :, cut].astype(F32)
                pieces = []
                for q in range(quarters):
                    pieces.append(ours[q * chunk_rows : (q + 1) * chunk_rows] * mis[level, q, :, cut])
                for side in range(2):
                    pieces.append(ph[side, i, :, cut] * mis_halo[level, side, :, cut])
                big, small = split(jnp.concatenate(pieces, axis=0))
                fs[u, 0:BLOCK, c : c + 128] = big
                fs[u, BLOCK : 2 * BLOCK, c : c + 128] = small
        for u, i in batch:
            to_modes(u, 2 * BLOCK, w1a)
        for u, i in batch:
            march(gb.at[u], hb.at[u], beta_v[level], first, last, columns)
            modes_out(u)
        for u, i in batch:
            for c in range(0, columns, wide):
                made = from_modes(u, w2a, c)
                out_v[i, :, c : c + wide] = alpha_v[i, :, c : c + wide] + (made[:rows] + made[rows:])
            pltpu.make_async_copy(out_v.at[i], out_hbm.at[u, level], out_sem.at[i]).start()
        return carry

    start_exchange()
    forward(0, 0, members)
    edges_sent(0)
    send_edges(1)
    send_sums(0)
    forward(1, 0, 2)
    send_halo_sums(0)
    forward(1, 2, members - 2)
    send_sums(1)
    send_halo_sums(1)
    swap_sums(0)
    send_misfit(0)
    swap_sums(1)
    send_misfit(1)
    take_misfit(0)
    take_halo(0)
    lax.fori_loop(0, 2, adjoint, 0)

    for i in range(fields):
        pltpu.make_async_copy(out_v.at[i], out_hbm.at[i % members, i // members], out_sem.at[i]).wait()
    edges_sent(1)
    for level in range(2):
        pair_copy(level).wait_send()
        for k in range(1, quarters):
            rs_copy(level, k).wait_send()
            ag_copy(level, k).wait_send()

        @pl.when(has_low)
        def _():
            rh_copy(level, 0).wait_send()

        @pl.when(has_high)
        def _():
            rh_copy(level, 1).wait_send()

        for there, side in ((at_low, 1), (at_high, 0)):

            @pl.when(there)
            def _():
                for p in range(quarters):
                    ah_copy(level, side, p).wait_send()


def local(tiles, groups, alpha, perturbations, innovation, obs_weight, diffusivity):
    members, levels, rows, columns = alpha.shape
    fields = members * levels
    w1f, w2f, w1a, w2a = transforms(rows)
    any_space = pl.BlockSpec(memory_space=pltpu.HBM)
    dma = pltpu.SemaphoreType.DMA
    quarters = groups // 2
    chunk = (rows // quarters, columns)
    halo = (HALO, columns)
    dense = (HALO, columns // 3 * 2)
    packed = -(-STEPS * members // 8) * 8
    made = pl.pallas_call(
        functools.partial(kernel, tiles, groups, members, rows, columns),
        out_shape=jax.ShapeDtypeStruct(alpha.shape, F32),
        in_specs=[pl.BlockSpec(memory_space=pltpu.SMEM)] + [any_space] * 8,
        out_specs=any_space,
        scratch_shapes=[
            pltpu.VMEM((fields, rows, columns), F32),
            pltpu.VMEM((fields, rows, columns), BF16),
            pltpu.VMEM((fields, rows, columns), F32),
            pltpu.VMEM((levels,) + chunk, F32),
            pltpu.VMEM((levels,) + chunk, F32),
            pltpu.VMEM(w1f.shape[1:], BF16),
            pltpu.VMEM(w2f.shape[1:], BF16),
            pltpu.VMEM(w1a.shape[1:], BF16),
            pltpu.VMEM(w2a.shape[1:], BF16),
            pltpu.VMEM((2, levels, packed, columns), F32),
            pltpu.VMEM((2, levels, packed, columns), F32),
            pltpu.VMEM((2, fields, HALO, columns), F32),
            pltpu.VMEM((fields, 2, HALO, columns), F32),
            pltpu.VMEM((levels, quarters) + chunk, F32),
            pltpu.VMEM((levels, 2) + dense, F32),
            pltpu.VMEM((levels, quarters) + chunk, F32),
            pltpu.VMEM((levels, quarters) + dense, F32),
            pltpu.VMEM((levels,) + chunk, F32),
            pltpu.VMEM((levels,) + chunk, F32),
            pltpu.VMEM((levels, quarters) + chunk, F32),
            pltpu.VMEM((levels, 2) + halo, F32),
            pltpu.VMEM((levels, 2) + dense, F32),
            pltpu.VMEM((levels, 2) + dense, F32),
            pltpu.VMEM((UNROLL, 2 * BLOCK, columns), BF16),
            pltpu.VMEM((UNROLL, PAD + 8 * RUN + PAD, BLOCK), F32),
            pltpu.VMEM((UNROLL, 8 * RUN, BLOCK), F32),
            pltpu.VMEM((UNROLL, 8 * RUN, 2 * BLOCK), BF16),
            pltpu.VMEM((levels, 8, BLOCK), F32),
            pltpu.VMEM((levels, 8, BLOCK), F32),
            dma((2, fields)),
            dma((6,)),
            dma((fields,)),
            dma((levels, 2)),
            dma((levels, 2)),
            dma((levels, quarters)),
            dma((levels, quarters)),
            dma((levels, 2)),
            dma((levels, quarters)),
            dma((levels,)),
            dma((levels,)),
            dma((levels, quarters)),
            dma((levels, quarters)),
            dma((levels, 2, quarters)),
            dma((levels, 2)),
        ],
        compiler_params=pltpu.CompilerParams(
            collective_id=0, has_side_effects=True, vmem_limit_bytes=60 * 2**20
        ),
    )(diffusivity, alpha, perturbations, innovation, obs_weight, w1f, w2f, w1a, w2a)
    return pl.pallas_call(
        pass_on,
        out_shape=jax.ShapeDtypeStruct(alpha.shape, F32),
        in_specs=[any_space],
        out_specs=any_space,
        scratch_shapes=[pltpu.VMEM(alpha.shape, F32), dma((2, fields))],
        compiler_params=pltpu.CompilerParams(vmem_limit_bytes=60 * 2**20),
    )(made)


def pass_on(src, dst, held, sem):
    fields = [(i, j) for i in range(src.shape[0]) for j in range(src.shape[1])]
    reads = [pltpu.make_async_copy(src.at[f], held.at[f], sem.at[0, n]) for n, f in enumerate(fields)]
    writes = [pltpu.make_async_copy(held.at[f], dst.at[f], sem.at[1, n]) for n, f in enumerate(fields)]
    for copy in reads:
        copy.start()
    for read, write in zip(reads, writes):
        read.wait()
        write.start()
    for copy in writes:
        copy.wait()


def solution(mesh):
    in_specs = (
        P("mem", None, "grid", None),
        P("mem", None, "grid", None),
        P(None, "grid", None),
        P(None, "grid", None),
        P(),
    )
    out_specs = P("mem", None, "grid", None)
    body = functools.partial(local, mesh.shape["grid"], mesh.shape["mem"])
    return jax.shard_map(body, mesh=mesh, in_specs=in_specs, out_specs=out_specs, check_vma=False)
```
